256 devices in a mesh: space: 4 (over y), energy: 64 (over x, z, core).
Axes of the slice: x: 4, y: 4, z: 8, core: 2. Of those that a mesh axis runs over, the one named last changes fastest.
Arguments:
- ham_blocks: float32 [4, 2, 256, 256], P('space'), may hold values from -0.1875 to 0.1875
- hopping: float32 [4, 2, 256, 256], P('space'), may hold values from -0.1875 to 0.1875
- energy: float32 [64], P('energy'), may hold values from -1.5 to 1.5
- broadening: float32 [64], P('energy'), may hold values from 0.05 to 0.2
- contact: float32 [64], P('energy'), may hold values from 0.5 to 2
- phonon_offset: int32 [64, 8], P('energy'), may hold values from -4 to 4, as said below
- phonon_weight: float32 [64, 8], P('energy'), may hold values from 0.1 to 0.4
Outputs:
- green: float32 [64, 4, 2, 256, 256], P('energy', 'space')
- self_energy: float32 [64, 4, 2, 256, 256], P('energy', 'space')
The draws below stay inside these ranges and needn't reach their ends.
Inputs may be any that keep to these rules, and one draw needn't show every extreme that they name: `phonon_offset`: for every energy, entry 0 is +4 and entry 1 is -4 (absorption and emission of the optical phonon); every other entry is nonzero with magnitude below 4.
All inputs are finite; a program needn't handle non-finite values.
Results may differ from the reference program's by a relative error of at most 0.00065.
Values sent between devices are 32-bit elements; how exact they have to be, the bound alone decides.
A program may use at most 128 MiB of HBM per device.

```python
import math
import jax
import jax.numpy as jnp
from jax import lax

B = 256
SHIFT = 4
PARTNERS = 8
NB = 4
NE = 64


def draw_phonon_offset(key, part):
    key_size, key_sign = jax.random.split(jax.random.fold_in(key, 17))
    magnitude = jax.random.randint(key_size, (NE, PARTNERS - 2), 1, SHIFT)
    polarity = 2 * jax.random.randint(key_sign, (NE, PARTNERS - 2), 0, 2) - 1
    optical = jnp.concatenate([jnp.full((NE, 1), SHIFT, jnp.int32), jnp.full((NE, 1), -SHIFT, jnp.int32)], 1)
    return jnp.concatenate([optical, (magnitude * polarity).astype(jnp.int32)], 1)


def block_scale(rng, extent, cuts, low, high):
    gain = 1.0
    for dim, parts in cuts:
        draws = jax.random.uniform(jax.random.fold_in(jax.random.fold_in(rng, 6), dim), (parts,), jnp.float32, low / len(cuts), high / len(cuts))
        gain = gain * jnp.repeat(jnp.exp(draws), extent[dim] // parts).reshape((-1,) + (1,) * (len(extent) - 1 - dim))
    return gain


def centred(stream_key, extent, deviation, most, cuts=(), kind=jnp.bfloat16):
    array = jax.random.normal(stream_key, extent, jnp.float32) * deviation
    if len(cuts) > 0:
        array = block_scale(stream_key, extent, cuts, -0.22, 0.18) * array
    return jnp.clip(array, min=-most, max=most).astype(kind)


def setup_inputs(seed: int = 0) -> dict:
    seeds = jax.random.split(jax.random.key(seed), 8)
    ham_blocks = centred(seeds[0], (NB, 2, B, B), (4 * B) ** -0.5, 0.1875, ((0, 4),), jnp.float32)
    hopping = centred(seeds[1], (NB, 2, B, B), (4 * B) ** -0.5, 0.1875, ((0, 4),), jnp.float32)
    energy = jnp.clip(jax.random.uniform(seeds[2], (NE,), jnp.float32, -1.5, 1.5) * block_scale(seeds[2], (NE,), ((0, 64),), -0.4, 0.0), -1.5, 1.5)
    broadening = jnp.clip(jnp.exp(math.log(0.2) - 1.3862944 * jax.random.uniform(seeds[3], (NE,), jnp.float32) ** block_scale(seeds[3], (NE,), ((0, 64),), -0.2, 0.2)), 0.05, 0.2)
    contact = jnp.clip(0.5 + 1.5 * jax.random.uniform(seeds[4], (NE,), jnp.float32) ** block_scale(seeds[4], (NE,), ((0, 64),), -0.2, 0.2), 0.5, 2.0)
    phonon_offset = draw_phonon_offset(jax.random.fold_in(seeds[7], 71), 0)
    phonon_weight = jnp.clip(0.1 + 0.3 * jax.random.uniform(seeds[6], (NE, PARTNERS), jnp.float32) ** block_scale(seeds[6], (NE, PARTNERS), ((0, 64),), -0.2, 0.2), 0.1, 0.4)
    return {"ham_blocks": ham_blocks, "hopping": hopping, "energy": energy, "broadening": broadening, "contact": contact, "phonon_offset": phonon_offset, "phonon_weight": phonon_weight}


highest = lax.Precision.HIGHEST

def complex_product(first_factor, second_factor):
    real_part = jnp.dot(first_factor[0], second_factor[0], precision=highest) - jnp.dot(first_factor[1], second_factor[1], precision=highest)
    imag_part = jnp.dot(first_factor[0], second_factor[1], precision=highest) + jnp.dot(first_factor[1], second_factor[0], precision=highest)
    return jnp.stack([real_part, imag_part])

def adjoint(matrix):
    return jnp.stack([matrix[0].T, -matrix[1].T])

def complex_inverse(matrix):
    block_order = matrix.shape[1]
    system = jnp.concatenate([jnp.concatenate([matrix[0], -matrix[1]], 1), jnp.concatenate([matrix[1], matrix[0]], 1)], 0)
    target = jnp.concatenate([jnp.eye(block_order, dtype=matrix.dtype), jnp.zeros((block_order, block_order), matrix.dtype)], 0)
    solved = jnp.linalg.solve(system, target)
    return jnp.stack([solved[:block_order], solved[block_order:]])

def reference(ham_blocks, hopping, energy, broadening, contact, phonon_offset, phonon_weight):
    flipped = jnp.stack([jnp.swapaxes(ham_blocks[:, 0], 1, 2), -jnp.swapaxes(ham_blocks[:, 1], 1, 2)], 1)
    hermitian = 0.5 * (ham_blocks + flipped)
    identity = jnp.eye(B, dtype=ham_blocks.dtype)
    naught = jnp.zeros((B, B), ham_blocks.dtype)
    lead_gram = complex_product(hopping[0], adjoint(hopping[0]))
    lead_term = jnp.stack([-lead_gram[1], lead_gram[0]])
    end_term = jnp.stack([naught, identity])

    def solve_energy(values):
        energy_level, damping, strength = values
        shifted = jnp.stack([energy_level * identity, damping * identity])
        blocks = shifted[None] - hermitian
        blocks = blocks.at[0].add(strength * lead_term)
        blocks = blocks.at[NB - 1].add(strength * end_term)
        vacant = jnp.stack([naught, naught])
        left_terms = [vacant]
        current = complex_inverse(blocks[0])
        for block_index in range(1, NB):
            sigma = complex_product(adjoint(hopping[block_index]), complex_product(current, hopping[block_index]))
            left_terms.append(sigma)
            current = complex_inverse(blocks[block_index] - sigma)
        right_terms = [vacant for block_index in range(NB)]
        current = complex_inverse(blocks[NB - 1])
        for block_index in range(NB - 2, -1, -1):
            sigma = complex_product(hopping[block_index + 1], complex_product(current, adjoint(hopping[block_index + 1])))
            right_terms[block_index] = sigma
            current = complex_inverse(blocks[block_index] - sigma)
        greens = [complex_inverse(blocks[block_index] - left_terms[block_index] - right_terms[block_index]) for block_index in range(NB)]
        return jnp.stack(greens)
    green = lax.map(solve_energy, (energy, broadening, contact))
    target = (jnp.arange(NE).astype(jnp.int32)[:, None] + phonon_offset).astype(jnp.int32)
    inside = (target >= 0) & (target < NE)
    clipped = jnp.clip(target, 0, NE - 1).astype(jnp.int32)
    weights_used = jnp.where(inside, phonon_weight, jnp.zeros_like(phonon_weight))

    def collect(values):
        partner_rows, scales = values
        picked = green[partner_rows]
        return jnp.sum(scales[:, None, None, None, None] * picked, axis=0)
    self_energy = lax.map(collect, (clipped, weights_used))
    return (green, self_energy)
```

```python
import functools

import jax
import jax.numpy as jnp
from jax import lax
from jax.experimental import pallas as pl
from jax.experimental.pallas import tpu as pltpu
from jax.sharding import PartitionSpec as P

SHIFT = 4
N = 256
SUB = 32
f32 = jnp.float32
bf16 = jnp.bfloat16
VREG = (8, 128)
SLOTS = 256


def passed_along(array, axis, by):
    peers = lax.axis_size(axis)
    pairs = [(i, i + by) for i in range(peers) if 0 <= i + by < peers]
    return lax.ppermute(array, axis, pairs)


def cmul(a, b):
    return (a[0] * b[0] - a[1] * b[1], a[0] * b[1] + a[1] * b[0])


def csub(a, b):
    return (a[0] - b[0], a[1] - b[1])


def cadd(a, b):
    return (a[0] + b[0], a[1] + b[1])


def lane_of(x, l):
    return tuple(jnp.broadcast_to(a[:, l : l + 1], VREG) for a in x)


def inv2(p00, p01, p10, p11):
    det = csub(cmul(p00, p11), cmul(p01, p10))
    d = 1.0 / (det[0] * det[0] + det[1] * det[1])
    q = (det[0] * d, -det[1] * d)
    return cmul(p11, q), cmul(p01, q), cmul(p10, q), cmul(p00, q)


class Rows:
    def __init__(self, ref):
        self.ref, self.next, self.kept = ref, 0, {}

    def __call__(self, x, j):
        out = []
        for a in x:
            if id(a) not in self.kept:
                slot = self.next
                self.next = (slot + 1) % SLOTS
                self.ref[slot * 8 : slot * 8 + 8, :] = a
                self.kept[id(a)] = (slot, a)
            slot = self.kept[id(a)][0]
            out.append(self.ref[pl.ds(slot * 8 + j, 8, stride=0), :])
        return tuple(out)


def eliminate_rows(W, t, o, rows_of):
    nv = len(W[0])
    ln = lax.broadcasted_iota(jnp.int32, VREG, 1)
    sb = lax.broadcasted_iota(jnp.int32, VREG, 0)
    el = lambda c, j: rows_of(c[j // 8], j % 8)
    c0 = {0: lane_of(W[t][0], o)}
    c1 = {0: lane_of(W[t][0], o + 1)}
    D = inv2(el(c0, 0), el(c1, 0), el(c0, 1), el(c1, 1))
    for j in range(0, 8 * nv, 2):
        l = o + j
        c0 = [lane_of(W[t][v], l) for v in range(nv)]
        c1 = [lane_of(W[t][v], l + 1) for v in range(nv)]
        i00, n01, n10, i11 = D
        ar = ln == l
        ab = ar | (ln == l + 1)
        new = []
        for s in range(2):
            r0 = rows_of(W[s][j // 8], j % 8)
            r1 = rows_of(W[s][(j + 1) // 8], (j + 1) % 8)
            if s == t:
                r0 = (jnp.where(ab, jnp.where(ar, 1.0, 0.0), r0[0]), jnp.where(ab, 0.0, r0[1]))
                r1 = (jnp.where(ab, jnp.where(ar, 0.0, 1.0), r1[0]), jnp.where(ab, 0.0, r1[1]))
            s0 = csub(cmul(i00, r0), cmul(n01, r1))
            s1 = csub(cmul(i11, r1), cmul(n10, r0))
            col = []
            for v in range(nv):
                X = W[s][v]
                if s == t:
                    X = (jnp.where(ab, 0.0, X[0]), jnp.where(ab, 0.0, X[1]))
                X = csub(X, cadd(cmul(c0[v], s0), cmul(c1[v], s1)))
                if j // 8 == v:
                    X = tuple(
                        jnp.where(sb == j % 8, s0[k], jnp.where(sb == j % 8 + 1, s1[k], X[k])) for k in range(2)
                    )
                col.append(X)
            new.append(col)
        if j + 2 < 8 * nv:
            vs = sorted({j // 8, (j + 2) // 8})
            pivot = []
            for ahead in (l + 2, l + 3):
                d = {v: lane_of(W[t][v], ahead) for v in vs}
                a, c = el(d, j), el(d, j + 1)
                s0 = csub(cmul(i00, a), cmul(n01, c))
                s1 = csub(cmul(i11, c), cmul(n10, a))
                for k in (j + 2, j + 3):
                    pivot.append(csub(el(d, k), cadd(cmul(el(c0, k), s0), cmul(el(c1, k), s1))))
            D = inv2(pivot[0], pivot[2], pivot[1], pivot[3])
        W = new
    return W


def halves(x):
    high = x.astype(bf16)
    return high, (x - high.astype(f32)).astype(bf16)


def dot(a, b):
    return jnp.dot(a, b, preferred_element_type=f32)


def stacked(parts, axis):
    return jnp.concatenate(parts, axis)


def left_panel(M, o):
    ln = lax.broadcasted_iota(jnp.int32, M[0].shape, 1)
    here = (ln >= o) & (ln < o + SUB)
    both = jnp.where(here, M[0], 0.0) + pltpu.roll(jnp.where(here, M[1], 0.0), SUB, 1)
    high = both.astype(bf16).astype(f32)
    low = both - high
    return stacked([(high + pltpu.roll(low, 2 * SUB, 1)).astype(bf16), high.astype(bf16)], 1)


def right_panel(W, o):
    re = stacked([stacked([W[s][v][0] for v in range(4)], 0) for s in range(2)], 1)
    im = stacked([stacked([W[s][v][1] for v in range(4)], 0) for s in range(2)], 1)
    (rh, rl), (ih, il) = halves(re), halves(im)
    top_h, bottom_h = stacked([rh, ih], 1), stacked([-ih, rh], 1)
    top_l, bottom_l = stacked([rl, il], 1), stacked([-il, rl], 1)
    none = jnp.zeros((SUB, 2 * N), bf16)
    first = [top_h, bottom_h, top_h, bottom_h]
    second = [top_l, bottom_l, none, none]
    turn = o // SUB
    around = lambda x: [x[(g - turn) % 4] for g in range(4)]
    return stacked(around(first) + around(second), 0)


def invert(mats, rows_of):
    def tile_steps(tile, carry):
        columns = [pl.ds(pl.multiple_of(128 * tile, 128), 128), pl.ds(pl.multiple_of(128 - 128 * tile, 128), 128)]
        rows_of.kept.clear()

        def rows(q, height):
            return pl.ds(pl.multiple_of(128 * tile + SUB * q, SUB), height)

        panels = []
        for M in mats:
            whole = [[M[k][rows(0, SUB), c] for k in range(2)] for c in columns]
            panels.append([[tuple(x[8 * v : 8 * v + 8] for x in w) for v in range(4)] for w in whole])
        ln = lax.broadcasted_iota(jnp.int32, (N, 128), 1)
        for q in range(4):
            o = q * SUB
            here = (ln >= o) & (ln < o + SUB)
            lefts = [left_panel([M[k][:, columns[0]] for k in range(2)], o) for M in mats]
            strips = [left_panel([M[k][rows((q + 1) % 4, SUB), columns[0]] for k in range(2)], o) for M in mats]
            panels = [eliminate_rows(W, 0, o, rows_of) for W in panels]
            following = []
            for M, L, W in zip(mats, lefts, panels):
                R = right_panel(W, o)
                if q < 3:
                    U = dot(strips.pop(0), R)
                    nxt = []
                    for s, c in enumerate(columns):
                        pairs = []
                        for k in range(2):
                            X = M[k][rows(q + 1, SUB), c]
                            if s == 0:
                                X = jnp.where(here[:SUB], 0.0, X)
                            pairs.append(X - U[:, k * N + s * 128 : k * N + s * 128 + 128])
                        nxt.append([tuple(x[8 * v : 8 * v + 8] for x in pairs) for v in range(4)])
                    following.append(nxt)
                U = dot(L, R)
                for s, c in enumerate(columns):
                    for k in range(2):
                        X = M[k][:, c]
                        if s == 0:
                            X = jnp.where(here, 0.0, X)
                        M[k][:, c] = X - U[:, k * N + s * 128 : k * N + s * 128 + 128]
                        M[k][rows(q, SUB), c] = stacked([W[s][v][k] for v in range(4)], 0)
            panels = following
        return carry

    lax.fori_loop(0, 2, tile_steps, 0)


def product(A, B):
    ah, al = halves(stacked([A[0], A[1]], 1))
    (rh, rl), (ih, il) = halves(B[0]), halves(B[1])
    bh = stacked([stacked([rh, ih], 1), stacked([-ih, rh], 1)], 0)
    bl = stacked([stacked([rl, il], 1), stacked([-il, rl], 1)], 0)
    C = dot(ah, bh) + (dot(ah, bl) + dot(al, bh))
    return C[:, :N], C[:, N:]


def planes(ref):
    return ref.at[0], ref.at[1]


def pair(ref):
    re, im = planes(ref)
    return re[...], im[...]


def put(ref, x):
    re, im = ref if isinstance(ref, tuple) else planes(ref)
    re[...], im[...] = x


def green_kernel(place_ref, level_ref, herm_ref, gram_ref, hop_ref, out_ref, outer, work, near, side_term, scr):
    rows_of = Rows(scr)
    place = place_ref[0]
    side = place // 2
    e, eta, c = level_ref[0], level_ref[1], level_ref[2]
    eye = (lax.broadcasted_iota(jnp.int32, (N, N), 0) == lax.broadcasted_iota(jnp.int32, (N, N), 1)).astype(f32)
    near_l, near_r = jnp.where(side == 0, 5, 3), jnp.where(side == 0, 1, 7)
    far_l, far_r = jnp.where(side == 0, 3, 5), jnp.where(side == 0, 7, 1)
    mid_l, mid_r = jnp.where(side == 0, 2, 6), jnp.where(side == 0, 6, 2)

    put(planes(outer.at[0]), (e * eye - herm_ref[0, 0] - c * gram_ref[1], eta * eye - herm_ref[0, 1] + c * gram_ref[0]))
    put(planes(outer.at[1]), (e * eye - herm_ref[3, 0], (eta + c) * eye - herm_ref[3, 1]))
    invert([planes(outer.at[0]), planes(outer.at[1])], rows_of)

    def inner(i, sigma):
        return (e * eye - herm_ref[i, 0] - sigma[0], eta * eye - herm_ref[i, 1] - sigma[1])

    right = product(pair(outer.at[side]), pair(hop_ref.at[near_r]))
    put(side_term, right)
    put(near, inner(1 + side, product(pair(hop_ref.at[near_l]), right)))
    right = product(pair(outer.at[1 - side]), pair(hop_ref.at[far_r]))
    put(work, inner(2 - side, product(pair(hop_ref.at[far_l]), right)))

    def solve(step, carry):
        invert([planes(work)], rows_of)

        @pl.when(step == 0)
        def _():
            right = product(pair(work), pair(hop_ref.at[mid_r]))
            put(work, csub(pair(near), product(pair(hop_ref.at[mid_l]), right)))

        return carry

    lax.fori_loop(0, 2, solve, 0)

    @pl.when((place == 1) | (place == 2))
    def _():
        put(out_ref, pair(work))

    @pl.when((place == 0) | (place == 3))
    def _():
        own = pair(outer.at[side])
        left = product(pair(hop_ref.at[near_l]), own)
        put(out_ref, cadd(own, product(pair(side_term), product(pair(work), left))))


def green_blocks(place, levels, herm, gram, hops):
    vmem = pl.BlockSpec(memory_space=pltpu.VMEM)
    smem = pl.BlockSpec(memory_space=pltpu.SMEM)
    block = pltpu.VMEM((2, N, N), f32)
    return pl.pallas_call(
        green_kernel,
        out_shape=jax.ShapeDtypeStruct((2, N, N), f32),
        in_specs=[smem, smem, vmem, vmem, vmem],
        out_specs=vmem,
        scratch_shapes=[pltpu.VMEM((2, 2, N, N), f32), block, block, block, pltpu.VMEM((8 * SLOTS, 128), f32)],
        compiler_params=pltpu.CompilerParams(vmem_limit_bytes=48 << 20),
        cost_estimate=pl.CostEstimate(flops=10**10, bytes_accessed=10**7, transcendentals=0),
    )(place, levels, herm, gram, hops)


def adjoint(x):
    return jnp.stack([jnp.swapaxes(x[..., 0, :, :], -1, -2), -jnp.swapaxes(x[..., 1, :, :], -1, -2)], -3)


def xproduct(a, b):
    d = functools.partial(jnp.dot, precision=lax.Precision.HIGHEST)
    return jnp.stack([d(a[0], b[0]) - d(a[1], b[1]), d(a[0], b[1]) + d(a[1], b[0])])


def per_device(ham_blocks, hopping, energy, broadening, contact, phonon_offset, phonon_weight):
    place = lax.axis_index("space").astype(jnp.int32).reshape(1)
    ham = lax.all_gather(ham_blocks[0], "space")
    hop = lax.all_gather(hopping[0], "space")
    herm = 0.5 * (ham + adjoint(ham))
    hops = jnp.concatenate([hop, adjoint(hop)], 0)
    gram = xproduct(hops[0], hops[4])
    levels = jnp.concatenate([energy, broadening, contact])
    green = green_blocks(place, levels, herm, gram, hops)
    offsets = phonon_offset[0]
    weights = phonon_weight[0]
    total = jnp.zeros_like(green)
    for offset in list(range(-SHIFT, 0)) + list(range(1, SHIFT + 1)):
        partner = passed_along(green, "energy", -offset)
        total = total + jnp.sum(jnp.where(offsets == offset, weights, jnp.zeros_like(weights))) * partner
    return (green[None, None], total[None, None])


def solution(mesh):
    placed = (
        P("space", None, None, None),
        P("space", None, None, None),
        P("energy"),
        P("energy"),
        P("energy"),
        P("energy", None),
        P("energy", None),
    )
    return jax.shard_map(
        per_device,
        mesh=mesh,
        in_specs=placed,
        out_specs=(P("energy", "space", None, None, None), P("energy", "space", None, None, None)),
        check_vma=False,
    )
```

```python
import functools

import jax
import jax.numpy as jnp
from jax import lax
from jax.experimental import pallas as pl
from jax.experimental.pallas import tpu as pltpu
from jax.sharding import PartitionSpec as P

N = 256
SUB = 32
f32 = jnp.float32
bf16 = jnp.bfloat16
VREG = (8, 128)
SLOTS = 256


CHUNKS = 4
PIECE = 512 // CHUNKS
MESH = pl.DeviceIdType.MESH


def greet(partners):
    barrier = pltpu.get_barrier_semaphore()
    for partner in partners:
        pl.semaphore_signal(barrier, inc=1, device_id=partner, device_id_type=MESH)
    pl.semaphore_wait(barrier, len(partners))


def gather_kernel(ham_ref, hop_ref, out_ref, herm, local_sem, send_sem, recv_sem):
    places = lax.axis_size("space")
    me = lax.axis_index("space")
    point = lax.axis_index("energy")
    core = lax.rem(point, 2)
    up, down = lax.rem(me + 1, places), lax.rem(me + places - 1, places)
    across = lax.rem(me + 2, places)
    above, below, beside = {"space": up}, {"space": down}, {"energy": point + 1 - 2 * core}
    greet((above, below, beside))
    rows = pl.ds(pl.multiple_of(128 * core, 128), 128)
    HERM, HOP = pl.ds(0, 2), pl.ds(2, 2)
    started = []

    def send(source, block, part, to, slot):
        copy = pltpu.make_async_remote_copy(
            src_ref=source,
            dst_ref=out_ref.at[block, part, rows],
            send_sem=send_sem.at[slot],
            recv_sem=recv_sem.at[slot],
            device_id=to,
            device_id_type=MESH,
        )
        copy.start()
        started.append(copy)
        return copy

    def pass_on(block, part, to, slot):
        return send(out_ref.at[block, part, rows], block, part, to, slot)

    hop_up = send(hop_ref.at[:, rows], me, HOP, above, 0)
    hop_down = send(hop_ref.at[:, rows], me, HOP, below, 1)
    herm[0] = 0.5 * (ham_ref[0] + ham_ref[0].T)
    herm[1] = 0.5 * (ham_ref[1] - ham_ref[1].T)
    herm_down = send(herm.at[:, rows], me, HERM, below, 2)
    herm_up = send(herm.at[:, rows], me, HERM, above, 3)
    own = [
        pltpu.make_async_copy(herm, out_ref.at[me, HERM], local_sem.at[0]),
        pltpu.make_async_copy(hop_ref, out_ref.at[me, HOP], local_sem.at[1]),
    ]
    for copy in own:
        copy.start()
    hop_up.wait_recv()
    hop_far = pass_on(down, HOP, above, 4)
    swaps = [pass_on(down, HOP, beside, 6)]
    hop_down.wait_recv()
    swaps.append(pass_on(up, HOP, beside, 7))
    herm_down.wait_recv()
    herm_far = pass_on(up, HERM, below, 5)
    swaps.append(pass_on(up, HERM, beside, 8))
    herm_up.wait_recv()
    swaps.append(pass_on(down, HERM, beside, 9))
    hop_far.wait_recv()
    swaps.append(pass_on(across, HOP, beside, 10))
    herm_far.wait_recv()
    swaps.append(pass_on(across, HERM, beside, 11))
    for copy in swaps:
        copy.wait_recv()
    for copy in started:
        copy.wait_send()
    for copy in own:
        copy.wait()


def gathered(ham, hop):
    vmem = pl.BlockSpec(memory_space=pltpu.VMEM)
    return pl.pallas_call(
        gather_kernel,
        out_shape=jax.ShapeDtypeStruct((4, 4, N, N), f32),
        in_specs=[vmem, vmem],
        out_specs=pl.BlockSpec(memory_space=pl.ANY),
        scratch_shapes=[
            pltpu.VMEM((2, N, N), f32),
            pltpu.SemaphoreType.DMA((2,)),
            pltpu.SemaphoreType.DMA((12,)),
            pltpu.SemaphoreType.DMA((12,)),
        ],
        compiler_params=pltpu.CompilerParams(collective_id=0, has_side_effects=True, vmem_limit_bytes=16 << 20),
        cost_estimate=pl.CostEstimate(flops=10**6, bytes_accessed=10**7, transcendentals=0),
    )(ham, hop)


def phonon_kernel(weight_ref, green_ref, out_ref, near, far, side, send_sem, recv_sem):
    points = lax.axis_size("energy")
    point = lax.axis_index("energy")
    core = lax.rem(point, 2)
    after, before = {"energy": lax.rem(point + 2, points)}, {"energy": lax.rem(point + points - 2, points)}
    beside = {"energy": point + 1 - 2 * core}
    along = (after, before)
    greet((after, before, beside))
    started = []

    def piece(i):
        return pl.ds(PIECE * i, PIECE)

    def send(source, target, to, slot):
        copy = pltpu.make_async_remote_copy(
            src_ref=source,
            dst_ref=target,
            send_sem=send_sem.at[slot],
            recv_sem=recv_sem.at[slot],
            device_id=to,
            device_id_type=MESH,
        )
        copy.start()
        started.append(copy)
        return copy

    def add(i, terms):
        total = out_ref[piece(i)]
        for k, ref in terms:
            total = total + weight_ref[k] * ref[piece(i)]
        out_ref[piece(i)] = total

    first, second, swap = {}, {}, {}
    for i in range(CHUNKS):
        for d in range(2):
            first[d, i] = send(green_ref.at[piece(i)], near.at[d, piece(i)], along[d], d * CHUNKS + i)
    for i in range(CHUNKS):
        swap[0, i] = send(green_ref.at[piece(i)], side.at[0, piece(i)], beside, 4 * CHUNKS + i)
    for i in range(CHUNKS):
        for d in range(2):
            first[d, i].wait_recv()
            second[d, i] = send(near.at[d, piece(i)], far.at[d, piece(i)], along[d], (2 + d) * CHUNKS + i)
            swap[1 + d, i] = send(near.at[d, piece(i)], side.at[1 + d, piece(i)], beside, (5 + d) * CHUNKS + i)
        swap[0, i].wait_recv()
        out_ref[piece(i)] = weight_ref[4] * side[0, piece(i)]
        add(i, [(0, near.at[0]), (1, near.at[1])])
    for i in range(CHUNKS):
        second[0, i].wait_recv()
        second[1, i].wait_recv()
        swap[3, i] = send(far.at[1 - core, piece(i)], side.at[3, piece(i)], beside, 7 * CHUNKS + i)
        swap[1, i].wait_recv()
        swap[2, i].wait_recv()
        add(i, [(2, far.at[0]), (3, far.at[1]), (5, side.at[1]), (6, side.at[2])])
    for i in range(CHUNKS):
        swap[3, i].wait_recv()
        add(i, [(7, side.at[3])])
    for copy in started:
        copy.wait_send()


def phonon_sum(weights, green):
    vmem = pl.BlockSpec(memory_space=pltpu.VMEM)
    block = (512, N)
    return pl.pallas_call(
        phonon_kernel,
        out_shape=jax.ShapeDtypeStruct(block, f32),
        in_specs=[pl.BlockSpec(memory_space=pltpu.SMEM), vmem],
        out_specs=vmem,
        scratch_shapes=[
            pltpu.VMEM((2, *block), f32),
            pltpu.VMEM((2, *block), f32),
            pltpu.VMEM((4, *block), f32),
            pltpu.SemaphoreType.DMA((8 * CHUNKS,)),
            pltpu.SemaphoreType.DMA((8 * CHUNKS,)),
        ],
        compiler_params=pltpu.CompilerParams(collective_id=1, has_side_effects=True, vmem_limit_bytes=24 << 20),
        cost_estimate=pl.CostEstimate(flops=10**6, bytes_accessed=10**7, transcendentals=0),
    )(weights, green)


def cmul(a, b):
    return (a[0] * b[0] - a[1] * b[1], a[0] * b[1] + a[1] * b[0])


def csub(a, b):
    return (a[0] - b[0], a[1] - b[1])


def cadd(a, b):
    return (a[0] + b[0], a[1] + b[1])


def lane_of(x, l):
    return tuple(jnp.broadcast_to(a[:, l : l + 1], VREG) for a in x)


def inv2(p00, p01, p10, p11):
    det = csub(cmul(p00, p11), cmul(p01, p10))
    d = 1.0 / (det[0] * det[0] + det[1] * det[1])
    q = (det[0] * d, -det[1] * d)
    return cmul(p11, q), cmul(p01, q), cmul(p10, q), cmul(p00, q)


class Rows:
    def __init__(self, ref):
        self.ref, self.next, self.kept = ref, 0, {}

    def __call__(self, x, j):
        out = []
        for a in x:
            if id(a) not in self.kept:
                slot = self.next
                self.next = (slot + 1) % SLOTS
                self.ref[slot * 8 : slot * 8 + 8, :] = a
                self.kept[id(a)] = (slot, a)
            slot = self.kept[id(a)][0]
            out.append(self.ref[pl.ds(slot * 8 + j, 8, stride=0), :])
        return tuple(out)


def eliminate_rows(W, t, o, rows_of):
    nv = len(W[0])
    ln = lax.broadcasted_iota(jnp.int32, VREG, 1)
    sb = lax.broadcasted_iota(jnp.int32, VREG, 0)
    el = lambda c, j: rows_of(c[j // 8], j % 8)
    c0 = {0: lane_of(W[t][0], o)}
    c1 = {0: lane_of(W[t][0], o + 1)}
    D = inv2(el(c0, 0), el(c1, 0), el(c0, 1), el(c1, 1))
    for j in range(0, 8 * nv, 2):
        l = o + j
        c0 = [lane_of(W[t][v], l) for v in range(nv)]
        c1 = [lane_of(W[t][v], l + 1) for v in range(nv)]
        i00, n01, n10, i11 = D
        ar = ln == l
        ab = ar | (ln == l + 1)
        new = []
        for s in range(2):
            r0 = rows_of(W[s][j // 8], j % 8)
            r1 = rows_of(W[s][(j + 1) // 8], (j + 1) % 8)
            if s == t:
                r0 = (jnp.where(ab, jnp.where(ar, 1.0, 0.0), r0[0]), jnp.where(ab, 0.0, r0[1]))
                r1 = (jnp.where(ab, jnp.where(ar, 0.0, 1.0), r1[0]), jnp.where(ab, 0.0, r1[1]))
            s0 = csub(cmul(i00, r0), cmul(n01, r1))
            s1 = csub(cmul(i11, r1), cmul(n10, r0))
            col = []
            for v in range(nv):
                X = W[s][v]
                if s == t:
                    X = (jnp.where(ab, 0.0, X[0]), jnp.where(ab, 0.0, X[1]))
                X = csub(X, cadd(cmul(c0[v], s0), cmul(c1[v], s1)))
                if j // 8 == v:
                    X = tuple(
                        jnp.where(sb == j % 8, s0[k], jnp.where(sb == j % 8 + 1, s1[k], X[k])) for k in range(2)
                    )
                col.append(X)
            new.append(col)
        if j + 2 < 8 * nv:
            vs = sorted({j // 8, (j + 2) // 8})
            pivot = []
            for ahead in (l + 2, l + 3):
                d = {v: lane_of(W[t][v], ahead) for v in vs}
                a, c = el(d, j), el(d, j + 1)
                s0 = csub(cmul(i00, a), cmul(n01, c))
                s1 = csub(cmul(i11, c), cmul(n10, a))
                for k in (j + 2, j + 3):
                    pivot.append(csub(el(d, k), cadd(cmul(el(c0, k), s0), cmul(el(c1, k), s1))))
            D = inv2(pivot[0], pivot[2], pivot[1], pivot[3])
        W = new
    return W


def halves(x):
    high = x.astype(bf16)
    return high, (x - high.astype(f32)).astype(bf16)


def dot(a, b):
    return jnp.dot(a, b, preferred_element_type=f32)


def stacked(parts, axis):
    return jnp.concatenate(parts, axis)


def left_panel(M, o):
    ln = lax.broadcasted_iota(jnp.int32, M[0].shape, 1)
    here = (ln >= o) & (ln < o + SUB)
    both = jnp.where(here, M[0], 0.0) + pltpu.roll(jnp.where(here, M[1], 0.0), SUB, 1)
    high = both.astype(bf16).astype(f32)
    low = both - high
    return stacked([(high + pltpu.roll(low, 2 * SUB, 1)).astype(bf16), high.astype(bf16)], 1)


def right_panel(W, o):
    re = stacked([stacked([W[s][v][0] for v in range(4)], 0) for s in range(2)], 1)
    im = stacked([stacked([W[s][v][1] for v in range(4)], 0) for s in range(2)], 1)
    (rh, rl), (ih, il) = halves(re), halves(im)
    top_h, bottom_h = stacked([rh, ih], 1), stacked([-ih, rh], 1)
    top_l, bottom_l = stacked([rl, il], 1), stacked([-il, rl], 1)
    none = jnp.zeros((SUB, 2 * N), bf16)
    first = [top_h, bottom_h, top_h, bottom_h]
    second = [top_l, bottom_l, none, none]
    turn = o // SUB
    around = lambda x: [x[(g - turn) % 4] for g in range(4)]
    return stacked(around(first) + around(second), 0)


def invert(mats, rows_of):
    def tile_steps(tile, carry):
        columns = [pl.ds(pl.multiple_of(128 * tile, 128), 128), pl.ds(pl.multiple_of(128 - 128 * tile, 128), 128)]
        rows_of.kept.clear()

        def rows(q, height):
            return pl.ds(pl.multiple_of(128 * tile + SUB * q, SUB), height)

        panels = []
        for M in mats:
            whole = [[M[k][rows(0, SUB), c] for k in range(2)] for c in columns]
            panels.append([[tuple(x[8 * v : 8 * v + 8] for x in w) for v in range(4)] for w in whole])
        ln = lax.broadcasted_iota(jnp.int32, (N, 128), 1)
        for q in range(4):
            o = q * SUB
            here = (ln >= o) & (ln < o + SUB)
            lefts = [left_panel([M[k][:, columns[0]] for k in range(2)], o) for M in mats]
            strips = [left_panel([M[k][rows((q + 1) % 4, SUB), columns[0]] for k in range(2)], o) for M in mats]
            panels = [eliminate_rows(W, 0, o, rows_of) for W in panels]
            following = []
            for M, L, W in zip(mats, lefts, panels):
                R = right_panel(W, o)
                if q < 3:
                    U = dot(strips.pop(0), R)
                    nxt = []
                    for s, c in enumerate(columns):
                        pairs = []
                        for k in range(2):
                            X = M[k][rows(q + 1, SUB), c]
                            if s == 0:
                                X = jnp.where(here[:SUB], 0.0, X)
                            pairs.append(X - U[:, k * N + s * 128 : k * N + s * 128 + 128])
                        nxt.append([tuple(x[8 * v : 8 * v + 8] for x in pairs) for v in range(4)])
                    following.append(nxt)
                U = dot(L, R)
                for s, c in enumerate(columns):
                    for k in range(2):
                        X = M[k][:, c]
                        if s == 0:
                            X = jnp.where(here, 0.0, X)
                        M[k][:, c] = X - U[:, k * N + s * 128 : k * N + s * 128 + 128]
                        M[k][rows(q, SUB), c] = stacked([W[s][v][k] for v in range(4)], 0)
            panels = following
        return carry

    lax.fori_loop(0, 2, tile_steps, 0)


def product(A, B):
    ah, al = halves(stacked([A[0], A[1]], 1))
    (rh, rl), (ih, il) = halves(B[0]), halves(B[1])
    bh = stacked([stacked([rh, ih], 1), stacked([-ih, rh], 1)], 0)
    bl = stacked([stacked([rl, il], 1), stacked([-il, rl], 1)], 0)
    C = dot(ah, bh) + (dot(ah, bl) + dot(al, bh))
    return C[:, :N], C[:, N:]


def planes(ref):
    return ref.at[0], ref.at[1]


def pair(ref):
    re, im = planes(ref)
    return re[...], im[...]


def put(ref, x):
    re, im = ref if isinstance(ref, tuple) else planes(ref)
    re[...], im[...] = x


def green_kernel(place_ref, level_ref, all_ref, out_ref, outer, work, near, side_term, lefts, scr):
    rows_of = Rows(scr)
    place = place_ref[0]
    side = place // 2
    e, eta, c = level_ref[0], level_ref[1], level_ref[2]
    eye = (lax.broadcasted_iota(jnp.int32, (N, N), 0) == lax.broadcasted_iota(jnp.int32, (N, N), 1)).astype(f32)
    herm = lambda k: (all_ref[k, 0], all_ref[k, 1])
    hop = lambda k: (all_ref[k, 2], all_ref[k, 3])
    back = lambda k: (all_ref[k, 2].T, -all_ref[k, 3].T)

    gram = product(hop(0), back(0))
    h0, h3 = herm(0), herm(3)
    put(planes(outer.at[0]), (e * eye - h0[0] - c * gram[1], eta * eye - h0[1] + c * gram[0]))
    put(planes(outer.at[1]), (e * eye - h3[0], (eta + c) * eye - h3[1]))
    put(planes(lefts.at[0]), back(1))
    put(planes(lefts.at[1]), hop(1))
    put(planes(lefts.at[2]), hop(3))
    put(planes(lefts.at[3]), back(3))

    @pl.when(side == 0)
    def _():
        put(planes(lefts.at[4]), hop(2))
        put(planes(lefts.at[5]), back(2))

    @pl.when(side == 1)
    def _():
        put(planes(lefts.at[4]), back(2))
        put(planes(lefts.at[5]), hop(2))

    invert([planes(outer.at[0]), planes(outer.at[1])], rows_of)

    def inner(i, sigma):
        h = herm(i)
        return (e * eye - h[0] - sigma[0], eta * eye - h[1] - sigma[1])

    far = 1 - side
    right = product(pair(outer.at[far]), pair(lefts.at[2 * far + 1]))
    put(work, inner(1 + far, product(pair(lefts.at[2 * far]), right)))
    right = product(pair(outer.at[side]), pair(lefts.at[2 * side + 1]))
    put(side_term, right)
    put(near, inner(1 + side, product(pair(lefts.at[2 * side]), right)))

    def solve(step, carry):
        invert([planes(work)], rows_of)

        @pl.when(step == 0)
        def _():
            right = product(pair(work), pair(lefts.at[5]))
            put(work, csub(pair(near), product(pair(lefts.at[4]), right)))

        return carry

    lax.fori_loop(0, 2, solve, 0)

    @pl.when((place == 1) | (place == 2))
    def _():
        put(out_ref, pair(work))

    @pl.when((place == 0) | (place == 3))
    def _():
        own = pair(outer.at[side])
        left = product(pair(lefts.at[2 * side]), own)
        put(out_ref, cadd(own, product(pair(side_term), product(pair(work), left))))


def green_block(place, levels, everything):
    vmem = pl.BlockSpec(memory_space=pltpu.VMEM)
    smem = pl.BlockSpec(memory_space=pltpu.SMEM)
    block = pltpu.VMEM((2, N, N), f32)
    return pl.pallas_call(
        green_kernel,
        out_shape=jax.ShapeDtypeStruct((2, N, N), f32),
        in_specs=[smem, smem, vmem],
        out_specs=vmem,
        scratch_shapes=[
            pltpu.VMEM((2, 2, N, N), f32),
            block,
            block,
            block,
            pltpu.VMEM((6, 2, N, N), f32),
            pltpu.VMEM((8 * SLOTS, 128), f32),
        ],
        compiler_params=pltpu.CompilerParams(vmem_limit_bytes=48 << 20),
        cost_estimate=pl.CostEstimate(flops=10**10, bytes_accessed=10**7, transcendentals=0),
    )(place, levels, everything)


def per_device(ham_blocks, hopping, energy, broadening, contact, phonon_offset, phonon_weight):
    place = lax.axis_index("space").astype(jnp.int32).reshape(1)
    point = lax.axis_index("energy").astype(jnp.int32)
    points = lax.axis_size("energy")
    everything = gathered(ham_blocks[0], hopping[0])
    green = green_block(place, jnp.concatenate([energy, broadening, contact]), everything)
    offsets, weights = phonon_offset[0], phonon_weight[0]
    inside = (point + offsets >= 0) & (point + offsets < points)
    even = point % 2 == 0
    reach = [-2, 2, -4, 4] + [jnp.where(even, a, b) for a, b in ((1, -1), (-1, -3), (3, 1), (-3, 3))]
    weight_of = jnp.stack([jnp.sum(jnp.where(inside & (offsets == d), weights, 0.0)) for d in reach])
    total = phonon_sum(weight_of, green.reshape(512, N)).reshape(2, N, N)
    return (green[None, None], total[None, None])


def solution(mesh):
    placed = (
        P("space", None, None, None),
        P("space", None, None, None),
        P("energy"),
        P("energy"),
        P("energy"),
        P("energy", None),
        P("energy", None),
    )
    return jax.shard_map(
        per_device,
        mesh=mesh,
        in_specs=placed,
        out_specs=(P("energy", "space", None, None, None), P("energy", "space", None, None, None)),
        check_vma=False,
    )
```

```python
import functools

import jax
import jax.numpy as jnp
from jax import lax
from jax.experimental import pallas as pl
from jax.experimental.pallas import tpu as pltpu
from jax.sharding import PartitionSpec as P

N = 256
SUB = 32
f32 = jnp.float32
bf16 = jnp.bfloat16
VREG = (8, 128)
SLOTS = 256


CHUNKS = 8
PIECE = 512 // CHUNKS
MESH = pl.DeviceIdType.MESH


def greet(partners):
    barrier = pltpu.get_barrier_semaphore()
    for partner in partners:
        pl.semaphore_signal(barrier, inc=1, device_id=partner, device_id_type=MESH)
    pl.semaphore_wait(barrier, len(partners))


def triangles():
    row = lax.broadcasted_iota(jnp.int32, (N, N), 0)
    column = lax.broadcasted_iota(jnp.int32, (N, N), 1)
    return row, column


def gather_kernel(ham_ref, hop_ref, herms_ref, hops_ref, ham, herm, local_sem, send_sem, recv_sem):
    places = lax.axis_size("space")
    me = lax.axis_index("space")
    point = lax.axis_index("energy")
    core = lax.rem(point, 2)
    up, down = lax.rem(me + 1, places), lax.rem(me + places - 1, places)
    across = lax.rem(me + 2, places)
    above, below, beside = {"space": up}, {"space": down}, {"energy": point + 1 - 2 * core}
    fetch = pltpu.make_async_copy(ham_ref, ham, local_sem.at[0])
    fetch.start()
    own = [pltpu.make_async_copy(hop_ref, hops_ref.at[me], local_sem.at[1])]
    own[0].start()
    greet((above, below, beside))
    rows = pl.ds(pl.multiple_of(128 * core, 128), 128)
    started = []
    herms_of = lambda k: herms_ref.at[k, rows]
    hops_of = lambda k, i: hops_ref.at[k, i, rows]

    def send(source, target, to, slot):
        copy = pltpu.make_async_remote_copy(
            src_ref=source,
            dst_ref=target,
            send_sem=send_sem.at[slot],
            recv_sem=recv_sem.at[slot],
            device_id=to,
            device_id_type=MESH,
        )
        copy.start()
        started.append(copy)
        return copy

    hop_up = [send(hop_ref.at[i, rows], hops_of(me, i), above, i) for i in (0, 1)]
    hop_down = [send(hop_ref.at[i, rows], hops_of(me, i), below, 2 + i) for i in (1, 0)][::-1]
    fetch.wait()
    row, column = triangles()
    herm[...] = 0.5 * jnp.where(row <= column, ham[0] + ham[0].T, ham[1] - ham[1].T)
    herm_up = send(herm.at[rows], herms_of(me), above, 4)
    herm_down = send(herm.at[rows], herms_of(me), below, 5)
    own.append(pltpu.make_async_copy(herm, herms_ref.at[me], local_sem.at[2]))
    own[1].start()
    hop_up[0].wait_recv()
    far_up = send(hops_of(down, 0), hops_of(down, 0), above, 6)
    swaps = [send(hops_of(down, 0), hops_of(down, 0), beside, 9)]
    hop_down[1].wait_recv()
    far_down = send(hops_of(up, 1), hops_of(up, 1), below, 7)
    swaps.append(send(hops_of(up, 1), hops_of(up, 1), beside, 10))
    hop_up[1].wait_recv()
    swaps.append(send(hops_of(down, 1), hops_of(down, 1), beside, 11))
    hop_down[0].wait_recv()
    swaps.append(send(hops_of(up, 0), hops_of(up, 0), beside, 12))
    half = 64
    top = pl.ds(pl.multiple_of(128 * core, 64), half)
    bottom = pl.ds(pl.multiple_of(128 * core + half, 64), half)
    herm_up.wait_recv()
    far_top = send(herms_ref.at[down, top], herms_ref.at[down, top], above, 8)
    swaps.append(send(herms_of(down), herms_of(down), beside, 13))
    herm_down.wait_recv()
    far_bottom = send(herms_ref.at[up, bottom], herms_ref.at[up, bottom], below, 14)
    swaps.append(send(herms_of(up), herms_of(up), beside, 15))
    far_up.wait_recv()
    swaps.append(send(hops_of(across, 0), hops_of(across, 0), beside, 16))
    far_down.wait_recv()
    swaps.append(send(hops_of(across, 1), hops_of(across, 1), beside, 17))
    far_top.wait_recv()
    swaps.append(send(herms_ref.at[across, top], herms_ref.at[across, top], beside, 18))
    far_bottom.wait_recv()
    swaps.append(send(herms_ref.at[across, bottom], herms_ref.at[across, bottom], beside, 19))
    for copy in swaps:
        copy.wait_recv()
    for copy in started:
        copy.wait_send()
    for copy in own:
        copy.wait()


def gathered(ham, hop):
    anywhere = pl.BlockSpec(memory_space=pl.ANY)
    return pl.pallas_call(
        gather_kernel,
        out_shape=(jax.ShapeDtypeStruct((4, N, N), f32), jax.ShapeDtypeStruct((4, 2, N, N), f32)),
        in_specs=[anywhere, anywhere],
        out_specs=(anywhere, anywhere),
        scratch_shapes=[
            pltpu.VMEM((2, N, N), f32),
            pltpu.VMEM((N, N), f32),
            pltpu.SemaphoreType.DMA((3,)),
            pltpu.SemaphoreType.DMA((20,)),
            pltpu.SemaphoreType.DMA((20,)),
        ],
        compiler_params=pltpu.CompilerParams(collective_id=0, has_side_effects=True, vmem_limit_bytes=16 << 20),
        cost_estimate=pl.CostEstimate(flops=10**6, bytes_accessed=10**7, transcendentals=0),
    )(ham, hop)


def phonon_kernel(weight_ref, green_ref, out_ref, near, far, side, send_sem, recv_sem):
    points = lax.axis_size("energy")
    point = lax.axis_index("energy")
    core = lax.rem(point, 2)
    after, before = {"energy": lax.rem(point + 2, points)}, {"energy": lax.rem(point + points - 2, points)}
    beside = {"energy": point + 1 - 2 * core}
    along = (after, before)
    greet((after, before, beside))
    started = []

    def piece(i):
        return pl.ds(PIECE * i, PIECE)

    def send(source, target, to, slot):
        copy = pltpu.make_async_remote_copy(
            src_ref=source,
            dst_ref=target,
            send_sem=send_sem.at[slot],
            recv_sem=recv_sem.at[slot],
            device_id=to,
            device_id_type=MESH,
        )
        copy.start()
        started.append(copy)
        return copy

    def add(i, terms):
        total = out_ref[piece(i)]
        for k, ref in terms:
            total = total + weight_ref[k] * ref[piece(i)]
        out_ref[piece(i)] = total

    first, second, swap = {}, {}, {}
    for i in range(CHUNKS):
        for d in range(2):
            first[d, i] = send(green_ref.at[piece(i)], near.at[d, piece(i)], along[d], d * CHUNKS + i)
    for i in range(CHUNKS):
        swap[0, i] = send(green_ref.at[piece(i)], side.at[0, piece(i)], beside, 4 * CHUNKS + i)
    for i in range(CHUNKS):
        for d in range(2):
            first[d, i].wait_recv()
            second[d, i] = send(near.at[d, piece(i)], far.at[d, piece(i)], along[d], (2 + d) * CHUNKS + i)
            swap[1 + d, i] = send(near.at[d, piece(i)], side.at[1 + d, piece(i)], beside, (5 + d) * CHUNKS + i)
        swap[0, i].wait_recv()
        out_ref[piece(i)] = weight_ref[4] * side[0, piece(i)]
        add(i, [(0, near.at[0]), (1, near.at[1])])
    for i in range(CHUNKS):
        second[0, i].wait_recv()
        second[1, i].wait_recv()
        swap[3, i] = send(far.at[1 - core, piece(i)], side.at[3, piece(i)], beside, 7 * CHUNKS + i)
        swap[1, i].wait_recv()
        swap[2, i].wait_recv()
        add(i, [(2, far.at[0]), (3, far.at[1]), (5, side.at[1]), (6, side.at[2])])
    for i in range(CHUNKS):
        swap[3, i].wait_recv()
        add(i, [(7, side.at[3])])
    for copy in started:
        copy.wait_send()


def phonon_sum(weights, green):
    vmem = pl.BlockSpec(memory_space=pltpu.VMEM)
    block = (512, N)
    return pl.pallas_call(
        phonon_kernel,
        out_shape=jax.ShapeDtypeStruct(block, f32),
        in_specs=[pl.BlockSpec(memory_space=pltpu.SMEM), vmem],
        out_specs=vmem,
        scratch_shapes=[
            pltpu.VMEM((2, *block), f32),
            pltpu.VMEM((2, *block), f32),
            pltpu.VMEM((4, *block), f32),
            pltpu.SemaphoreType.DMA((8 * CHUNKS,)),
            pltpu.SemaphoreType.DMA((8 * CHUNKS,)),
        ],
        compiler_params=pltpu.CompilerParams(collective_id=1, has_side_effects=True, vmem_limit_bytes=24 << 20),
        cost_estimate=pl.CostEstimate(flops=10**6, bytes_accessed=10**7, transcendentals=0),
    )(weights, green)


def cmul(a, b):
    return (a[0] * b[0] - a[1] * b[1], a[0] * b[1] + a[1] * b[0])


def csub(a, b):
    return (a[0] - b[0], a[1] - b[1])


def cadd(a, b):
    return (a[0] + b[0], a[1] + b[1])


def lane_of(x, l):
    return tuple(jnp.broadcast_to(a[:, l : l + 1], VREG) for a in x)


def inv2(p00, p01, p10, p11):
    det = csub(cmul(p00, p11), cmul(p01, p10))
    d = 1.0 / (det[0] * det[0] + det[1] * det[1])
    q = (det[0] * d, -det[1] * d)
    return cmul(p11, q), cmul(p01, q), cmul(p10, q), cmul(p00, q)


class Rows:
    def __init__(self, ref):
        self.ref, self.next, self.kept = ref, 0, {}

    def __call__(self, x, j):
        out = []
        for a in x:
            if id(a) not in self.kept:
                slot = self.next
                self.next = (slot + 1) % SLOTS
                self.ref[slot * 8 : slot * 8 + 8, :] = a
                self.kept[id(a)] = (slot, a)
            slot = self.kept[id(a)][0]
            out.append(self.ref[pl.ds(slot * 8 + j, 8, stride=0), :])
        return tuple(out)


def eliminate_rows(W, t, o, rows_of):
    nv = len(W[0])
    ln = lax.broadcasted_iota(jnp.int32, VREG, 1)
    sb = lax.broadcasted_iota(jnp.int32, VREG, 0)
    el = lambda c, j: rows_of(c[j // 8], j % 8)
    c0 = [lane_of(W[t][v], o) for v in range(nv)]
    c1 = [lane_of(W[t][v], o + 1) for v in range(nv)]
    D = inv2(el(c0, 0), el(c1, 0), el(c0, 1), el(c1, 1))
    for j in range(0, 8 * nv, 2):
        l = o + j
        i00, n01, n10, i11 = D
        ar = ln == l
        ab = ar | (ln == l + 1)

        def rows_in(v, X, s0, s1):
            if j // 8 != v:
                return X
            return tuple(jnp.where(sb == j % 8, s0[k], jnp.where(sb == j % 8 + 1, s1[k], X[k])) for k in range(2))

        last = j + 2 == 8 * nv
        if not last:
            nxt, pivot = [], []
            for ahead in (l + 2, l + 3):
                d = [lane_of(W[t][v], ahead) for v in range(nv)]
                a, c = el(d, j), el(d, j + 1)
                s0 = csub(cmul(i00, a), cmul(n01, c))
                s1 = csub(cmul(i11, c), cmul(n10, a))
                for k in (j + 2, j + 3):
                    pivot.append(csub(el(d, k), cadd(cmul(el(c0, k), s0), cmul(el(c1, k), s1))))
                nxt.append(
                    [rows_in(v, csub(d[v], cadd(cmul(c0[v], s0), cmul(c1[v], s1))), s0, s1) for v in range(nv)]
                )
            D = inv2(pivot[0], pivot[2], pivot[1], pivot[3])
        new = []
        for s in range(2):
            r0 = rows_of(W[s][j // 8], j % 8)
            r1 = rows_of(W[s][(j + 1) // 8], (j + 1) % 8)
            if s == t:
                r0 = (jnp.where(ab, jnp.where(ar, 1.0, 0.0), r0[0]), jnp.where(ab, 0.0, r0[1]))
                r1 = (jnp.where(ab, jnp.where(ar, 0.0, 1.0), r1[0]), jnp.where(ab, 0.0, r1[1]))
            s0 = csub(cmul(i00, r0), cmul(n01, r1))
            s1 = csub(cmul(i11, r1), cmul(n10, r0))
            col = []
            for v in range(nv):
                X = W[s][v]
                if s == t:
                    X = (jnp.where(ab, 0.0, X[0]), jnp.where(ab, 0.0, X[1]))
                col.append(rows_in(v, csub(X, cadd(cmul(c0[v], s0), cmul(c1[v], s1))), s0, s1))
            new.append(col)
        W = new
        if not last:
            c0, c1 = nxt
    return W


def halves(x):
    high = x.astype(bf16)
    return high, (x - high.astype(f32)).astype(bf16)


def dot(a, b):
    return jnp.dot(a, b, preferred_element_type=f32)


def stacked(parts, axis):
    return jnp.concatenate(parts, axis)


def left_panel(M, o):
    ln = lax.broadcasted_iota(jnp.int32, M[0].shape, 1)
    here = (ln >= o) & (ln < o + SUB)
    both = jnp.where(here, M[0], 0.0) + pltpu.roll(jnp.where(here, M[1], 0.0), SUB, 1)
    high = both.astype(bf16).astype(f32)
    low = both - high
    return stacked([(high + pltpu.roll(low, 2 * SUB, 1)).astype(bf16), high.astype(bf16)], 1)


def right_panel(W, o):
    re = stacked([stacked([W[s][v][0] for v in range(4)], 0) for s in range(2)], 1)
    im = stacked([stacked([W[s][v][1] for v in range(4)], 0) for s in range(2)], 1)
    (rh, rl), (ih, il) = halves(re), halves(im)
    top_h, bottom_h = stacked([rh, ih], 1), stacked([-ih, rh], 1)
    top_l, bottom_l = stacked([rl, il], 1), stacked([-il, rl], 1)
    none = jnp.zeros((SUB, 2 * N), bf16)
    first = [top_h, bottom_h, top_h, bottom_h]
    second = [top_l, bottom_l, none, none]
    turn = o // SUB
    around = lambda x: [x[(g - turn) % 4] for g in range(4)]
    return stacked(around(first) + around(second), 0)


def invert(mats, rows_of):
    def tile_steps(tile, carry):
        columns = [pl.ds(pl.multiple_of(128 * tile, 128), 128), pl.ds(pl.multiple_of(128 - 128 * tile, 128), 128)]
        rows_of.kept.clear()

        def rows(q, height):
            return pl.ds(pl.multiple_of(128 * tile + SUB * q, SUB), height)

        panels = []
        for M in mats:
            whole = [[M[k][rows(0, SUB), c] for k in range(2)] for c in columns]
            panels.append([[tuple(x[8 * v : 8 * v + 8] for x in w) for v in range(4)] for w in whole])
        ln = lax.broadcasted_iota(jnp.int32, (N, 128), 1)
        for q in range(4):
            o = q * SUB
            here = (ln >= o) & (ln < o + SUB)
            lefts = [left_panel([M[k][:, columns[0]] for k in range(2)], o) for M in mats]
            strips = [left_panel([M[k][rows((q + 1) % 4, SUB), columns[0]] for k in range(2)], o) for M in mats]
            panels = [eliminate_rows(W, 0, o, rows_of) for W in panels]
            following = []
            for M, L, W in zip(mats, lefts, panels):
                R = right_panel(W, o)
                if q < 3:
                    U = dot(strips.pop(0), R)
                    nxt = []
                    for s, c in enumerate(columns):
                        pairs = []
                        for k in range(2):
                            X = M[k][rows(q + 1, SUB), c]
                            if s == 0:
                                X = jnp.where(here[:SUB], 0.0, X)
                            pairs.append(X - U[:, k * N + s * 128 : k * N + s * 128 + 128])
                        nxt.append([tuple(x[8 * v : 8 * v + 8] for x in pairs) for v in range(4)])
                    following.append(nxt)
                U = dot(L, R)
                for s, c in enumerate(columns):
                    for k in range(2):
                        X = M[k][:, c]
                        if s == 0:
                            X = jnp.where(here, 0.0, X)
                        M[k][:, c] = X - U[:, k * N + s * 128 : k * N + s * 128 + 128]
                        M[k][rows(q, SUB), c] = stacked([W[s][v][k] for v in range(4)], 0)
            panels = following
        return carry

    lax.fori_loop(0, 2, tile_steps, 0)


def product(A, B):
    ah, al = halves(stacked([A[0], A[1]], 1))
    (rh, rl), (ih, il) = halves(B[0]), halves(B[1])
    bh = stacked([stacked([rh, ih], 1), stacked([-ih, rh], 1)], 0)
    bl = stacked([stacked([rl, il], 1), stacked([-il, rl], 1)], 0)
    C = dot(ah, bh) + (dot(ah, bl) + dot(al, bh))
    return C[:, :N], C[:, N:]


def planes(ref):
    return ref.at[0], ref.at[1]


def pair(ref):
    re, im = planes(ref)
    return re[...], im[...]


def put(ref, x):
    re, im = ref if isinstance(ref, tuple) else planes(ref)
    re[...], im[...] = x


def green_kernel(
    energy_ref, broadening_ref, contact_ref, offset_ref, weight_ref, herm_ref, hop_ref, out_ref, reach_ref,
    outer, work, near, side_term, lefts, scr,
):
    rows_of = Rows(scr)
    place = lax.axis_index("space")
    point, points = lax.axis_index("energy"), lax.axis_size("energy")
    side = place // 2
    e, eta, c = energy_ref[0], broadening_ref[0], contact_ref[0]

    even = lax.rem(point, 2) == 0
    reach = [-2, 2, -4, 4] + [jnp.where(even, a, b) for a, b in ((1, -1), (-1, -3), (3, 1), (-3, 3))]
    for k, d in enumerate(reach):
        inside = (point + d >= 0) & (point + d < points)
        total = jnp.float32(0.0)
        for j in range(8):
            total = total + jnp.where(inside & (offset_ref[0, j] == d), weight_ref[0, j], 0.0)
        reach_ref[k] = total

    row, column = triangles()
    eye = (row == column).astype(f32)

    def herm(k):
        mixed = herm_ref[k]
        turned = mixed.T
        return (
            jnp.where(row <= column, mixed, turned),
            jnp.where(row > column, mixed, jnp.where(row < column, -turned, 0.0)),
        )

    hop = lambda k: (hop_ref[k, 0], hop_ref[k, 1])
    back = lambda k: (hop_ref[k, 0].T, -hop_ref[k, 1].T)

    gram = product(hop(0), back(0))
    h0, h3 = herm(0), herm(3)
    put(planes(outer.at[0]), (e * eye - h0[0] - c * gram[1], eta * eye - h0[1] + c * gram[0]))
    put(planes(outer.at[1]), (e * eye - h3[0], (eta + c) * eye - h3[1]))
    put(planes(lefts.at[0]), back(1))
    put(planes(lefts.at[1]), hop(1))
    put(planes(lefts.at[2]), hop(3))
    put(planes(lefts.at[3]), back(3))

    @pl.when(side == 0)
    def _():
        put(planes(lefts.at[4]), hop(2))
        put(planes(lefts.at[5]), back(2))

    @pl.when(side == 1)
    def _():
        put(planes(lefts.at[4]), back(2))
        put(planes(lefts.at[5]), hop(2))

    invert([planes(outer.at[0]), planes(outer.at[1])], rows_of)

    def inner(i, sigma):
        h = herm(i)
        return (e * eye - h[0] - sigma[0], eta * eye - h[1] - sigma[1])

    far = 1 - side
    right = product(pair(outer.at[far]), pair(lefts.at[2 * far + 1]))
    put(work, inner(1 + far, product(pair(lefts.at[2 * far]), right)))
    right = product(pair(outer.at[side]), pair(lefts.at[2 * side + 1]))
    put(side_term, right)
    put(near, inner(1 + side, product(pair(lefts.at[2 * side]), right)))

    def solve(step, carry):
        invert([planes(work)], rows_of)

        @pl.when(step == 0)
        def _():
            right = product(pair(work), pair(lefts.at[5]))
            put(work, csub(pair(near), product(pair(lefts.at[4]), right)))

        return carry

    lax.fori_loop(0, 2, solve, 0)

    @pl.when((place == 1) | (place == 2))
    def _():
        put(out_ref, pair(work))

    @pl.when((place == 0) | (place == 3))
    def _():
        own = pair(outer.at[side])
        left = product(pair(lefts.at[2 * side]), own)
        put(out_ref, cadd(own, product(pair(side_term), product(pair(work), left))))


def green_block(energy, broadening, contact, offset, weight, herms, hops):
    vmem = pl.BlockSpec(memory_space=pltpu.VMEM)
    smem = pl.BlockSpec(memory_space=pltpu.SMEM)
    block = pltpu.VMEM((2, N, N), f32)
    return pl.pallas_call(
        green_kernel,
        out_shape=(jax.ShapeDtypeStruct((2, N, N), f32), jax.ShapeDtypeStruct((8,), f32)),
        in_specs=[smem] * 5 + [vmem] * 2,
        out_specs=(vmem, smem),
        scratch_shapes=[
            pltpu.VMEM((2, 2, N, N), f32),
            block,
            block,
            block,
            pltpu.VMEM((6, 2, N, N), f32),
            pltpu.VMEM((8 * SLOTS, 128), f32),
        ],
        compiler_params=pltpu.CompilerParams(vmem_limit_bytes=48 << 20),
        cost_estimate=pl.CostEstimate(flops=10**10, bytes_accessed=10**7, transcendentals=0),
    )(energy, broadening, contact, offset, weight, herms, hops)


def per_device(ham_blocks, hopping, energy, broadening, contact, phonon_offset, phonon_weight):
    herms, hops = gathered(ham_blocks[0], hopping[0])
    green, reach = green_block(energy, broadening, contact, phonon_offset, phonon_weight, herms, hops)
    total = phonon_sum(reach, green.reshape(512, N)).reshape(2, N, N)
    return (green[None, None], total[None, None])


def solution(mesh):
    placed = (
        P("space", None, None, None),
        P("space", None, None, None),
        P("energy"),
        P("energy"),
        P("energy"),
        P("energy", None),
        P("energy", None),
    )
    return jax.shard_map(
        per_device,
        mesh=mesh,
        in_specs=placed,
        out_specs=(P("energy", "space", None, None, None), P("energy", "space", None, None, None)),
        check_vma=False,
    )
```

```python
import functools

import jax
import jax.numpy as jnp
from jax import lax
from jax.experimental import pallas as pl
from jax.experimental.pallas import tpu as pltpu
from jax.sharding import PartitionSpec as P

N = 256
SUB = 32
f32 = jnp.float32
bf16 = jnp.bfloat16
VREG = (8, 128)
SLOTS = 256


CHUNKS = 8
PIECE = 512 // CHUNKS
MESH = pl.DeviceIdType.MESH


def greet(partners):
    barrier = pltpu.get_barrier_semaphore()
    for partner in partners:
        pl.semaphore_signal(barrier, inc=1, device_id=partner, device_id_type=MESH)
    pl.semaphore_wait(barrier, len(partners))


def triangles():
    row = lax.broadcasted_iota(jnp.int32, (N, N), 0)
    column = lax.broadcasted_iota(jnp.int32, (N, N), 1)
    return row, column


def gather_kernel(ham_ref, hop_ref, herms_ref, hops_ref, ham, herm, local_sem, send_sem, recv_sem):
    places = lax.axis_size("space")
    me = lax.axis_index("space")
    point = lax.axis_index("energy")
    core = lax.rem(point, 2)
    up, down = lax.rem(me + 1, places), lax.rem(me + places - 1, places)
    across = lax.rem(me + 2, places)
    above, below, beside = {"space": up}, {"space": down}, {"energy": point + 1 - 2 * core}
    fetch = pltpu.make_async_copy(ham_ref, ham, local_sem.at[0])
    fetch.start()
    own = [pltpu.make_async_copy(hop_ref, hops_ref.at[me], local_sem.at[1])]
    own[0].start()
    greet((above, below, beside))
    rows = pl.ds(pl.multiple_of(128 * core, 128), 128)
    started = []
    herms_of = lambda k: herms_ref.at[k, rows]
    hops_of = lambda k, i: hops_ref.at[k, i, rows]

    def send(source, target, to, slot):
        copy = pltpu.make_async_remote_copy(
            src_ref=source,
            dst_ref=target,
            send_sem=send_sem.at[slot],
            recv_sem=recv_sem.at[slot],
            device_id=to,
            device_id_type=MESH,
        )
        copy.start()
        started.append(copy)
        return copy

    hop_up = [send(hop_ref.at[i, rows], hops_of(me, i), above, i) for i in (0, 1)]
    hop_down = [send(hop_ref.at[i, rows], hops_of(me, i), below, 2 + i) for i in (1, 0)][::-1]
    fetch.wait()
    row, column = triangles()
    herm[...] = 0.5 * jnp.where(row <= column, ham[0] + ham[0].T, ham[1] - ham[1].T)
    herm_up = send(herm.at[rows], herms_of(me), above, 4)
    herm_down = send(herm.at[rows], herms_of(me), below, 5)
    own.append(pltpu.make_async_copy(herm, herms_ref.at[me], local_sem.at[2]))
    own[1].start()
    hop_up[0].wait_recv()
    far_up = send(hops_of(down, 0), hops_of(down, 0), above, 6)
    swaps = [send(hops_of(down, 0), hops_of(down, 0), beside, 9)]
    hop_down[1].wait_recv()
    far_down = send(hops_of(up, 1), hops_of(up, 1), below, 7)
    swaps.append(send(hops_of(up, 1), hops_of(up, 1), beside, 10))
    hop_up[1].wait_recv()
    swaps.append(send(hops_of(down, 1), hops_of(down, 1), beside, 11))
    hop_down[0].wait_recv()
    swaps.append(send(hops_of(up, 0), hops_of(up, 0), beside, 12))
    half = 64
    top = pl.ds(pl.multiple_of(128 * core, 64), half)
    bottom = pl.ds(pl.multiple_of(128 * core + half, 64), half)
    herm_up.wait_recv()
    far_top = send(herms_ref.at[down, top], herms_ref.at[down, top], above, 8)
    swaps.append(send(herms_of(down), herms_of(down), beside, 13))
    herm_down.wait_recv()
    far_bottom = send(herms_ref.at[up, bottom], herms_ref.at[up, bottom], below, 14)
    swaps.append(send(herms_of(up), herms_of(up), beside, 15))
    far_up.wait_recv()
    swaps.append(send(hops_of(across, 0), hops_of(across, 0), beside, 16))
    far_down.wait_recv()
    swaps.append(send(hops_of(across, 1), hops_of(across, 1), beside, 17))
    far_top.wait_recv()
    swaps.append(send(herms_ref.at[across, top], herms_ref.at[across, top], beside, 18))
    far_bottom.wait_recv()
    swaps.append(send(herms_ref.at[across, bottom], herms_ref.at[across, bottom], beside, 19))
    for copy in swaps:
        copy.wait_recv()
    for copy in started:
        copy.wait_send()
    for copy in own:
        copy.wait()


def gathered(ham, hop):
    anywhere = pl.BlockSpec(memory_space=pl.ANY)
    return pl.pallas_call(
        gather_kernel,
        out_shape=(jax.ShapeDtypeStruct((4, N, N), f32), jax.ShapeDtypeStruct((4, 2, N, N), f32)),
        in_specs=[pl.BlockSpec(memory_space=pltpu.HBM)] * 2,
        out_specs=(anywhere, anywhere),
        scratch_shapes=[
            pltpu.VMEM((2, N, N), f32),
            pltpu.VMEM((N, N), f32),
            pltpu.SemaphoreType.DMA((3,)),
            pltpu.SemaphoreType.DMA((20,)),
            pltpu.SemaphoreType.DMA((20,)),
        ],
        compiler_params=pltpu.CompilerParams(collective_id=0, has_side_effects=True, vmem_limit_bytes=16 << 20),
        cost_estimate=pl.CostEstimate(flops=10**6, bytes_accessed=10**7, transcendentals=0),
    )(ham, hop)


def phonon_kernel(weight_ref, green_ref, out_ref, near, far, side, send_sem, recv_sem):
    points = lax.axis_size("energy")
    point = lax.axis_index("energy")
    core = lax.rem(point, 2)
    after, before = {"energy": lax.rem(point + 2, points)}, {"energy": lax.rem(point + points - 2, points)}
    beside = {"energy": point + 1 - 2 * core}
    along = (after, before)
    greet((after, before, beside))
    started = []

    def piece(i):
        return pl.ds(PIECE * i, PIECE)

    def send(source, target, to, slot):
        copy = pltpu.make_async_remote_copy(
            src_ref=source,
            dst_ref=target,
            send_sem=send_sem.at[slot],
            recv_sem=recv_sem.at[slot],
            device_id=to,
            device_id_type=MESH,
        )
        copy.start()
        started.append(copy)
        return copy

    def add(i, terms):
        total = out_ref[piece(i)]
        for k, ref in terms:
            total = total + weight_ref[k] * ref[piece(i)]
        out_ref[piece(i)] = total

    first, second, swap = {}, {}, {}
    for i in range(CHUNKS):
        for d in range(2):
            first[d, i] = send(green_ref.at[piece(i)], near.at[d, piece(i)], along[d], d * CHUNKS + i)
    for i in range(CHUNKS):
        swap[0, i] = send(green_ref.at[piece(i)], side.at[0, piece(i)], beside, 4 * CHUNKS + i)
    for i in range(CHUNKS):
        for d in range(2):
            first[d, i].wait_recv()
            second[d, i] = send(near.at[d, piece(i)], far.at[d, piece(i)], along[d], (2 + d) * CHUNKS + i)
            swap[1 + d, i] = send(near.at[d, piece(i)], side.at[1 + d, piece(i)], beside, (5 + d) * CHUNKS + i)
        swap[0, i].wait_recv()
        out_ref[piece(i)] = weight_ref[4] * side[0, piece(i)]
        add(i, [(0, near.at[0]), (1, near.at[1])])
    for i in range(CHUNKS):
        second[0, i].wait_recv()
        second[1, i].wait_recv()
        swap[3, i] = send(far.at[1 - core, piece(i)], side.at[3, piece(i)], beside, 7 * CHUNKS + i)
        swap[1, i].wait_recv()
        swap[2, i].wait_recv()
        add(i, [(2, far.at[0]), (3, far.at[1]), (5, side.at[1]), (6, side.at[2])])
    for i in range(CHUNKS):
        swap[3, i].wait_recv()
        add(i, [(7, side.at[3])])
    for copy in started:
        copy.wait_send()


def phonon_sum(weights, green):
    vmem = pl.BlockSpec(memory_space=pltpu.VMEM)
    block = (512, N)
    return pl.pallas_call(
        phonon_kernel,
        out_shape=jax.ShapeDtypeStruct(block, f32),
        in_specs=[pl.BlockSpec(memory_space=pltpu.SMEM), pl.BlockSpec(memory_space=pltpu.HBM)],
        out_specs=vmem,
        scratch_shapes=[
            pltpu.VMEM((2, *block), f32),
            pltpu.VMEM((2, *block), f32),
            pltpu.VMEM((4, *block), f32),
            pltpu.SemaphoreType.DMA((8 * CHUNKS,)),
            pltpu.SemaphoreType.DMA((8 * CHUNKS,)),
        ],
        compiler_params=pltpu.CompilerParams(collective_id=1, has_side_effects=True, vmem_limit_bytes=24 << 20),
        cost_estimate=pl.CostEstimate(flops=10**6, bytes_accessed=10**7, transcendentals=0),
    )(weights, green)


def cmul(a, b):
    return (a[0] * b[0] - a[1] * b[1], a[0] * b[1] + a[1] * b[0])


def csub(a, b):
    return (a[0] - b[0], a[1] - b[1])


def cadd(a, b):
    return (a[0] + b[0], a[1] + b[1])


def lane_of(x, l):
    return tuple(jnp.broadcast_to(a[:, l : l + 1], VREG) for a in x)


def inv2(p00, p01, p10, p11):
    det = csub(cmul(p00, p11), cmul(p01, p10))
    d = 1.0 / (det[0] * det[0] + det[1] * det[1])
    q = (det[0] * d, -det[1] * d)
    return cmul(p11, q), cmul(p01, q), cmul(p10, q), cmul(p00, q)


class Rows:
    def __init__(self, ref):
        self.ref, self.next, self.kept = ref, 0, {}

    def __call__(self, x, j):
        out = []
        for a in x:
            if id(a) not in self.kept:
                slot = self.next
                self.next = (slot + 1) % SLOTS
                self.ref[slot * 8 : slot * 8 + 8, :] = a
                self.kept[id(a)] = (slot, a)
            slot = self.kept[id(a)][0]
            out.append(self.ref[pl.ds(slot * 8 + j, 8, stride=0), :])
        return tuple(out)


def eliminate_rows(W, t, o, rows_of):
    nv = len(W[0])
    ln = lax.broadcasted_iota(jnp.int32, VREG, 1)
    sb = lax.broadcasted_iota(jnp.int32, VREG, 0)
    el = lambda c, j: rows_of(c[j // 8], j % 8)
    c0 = [lane_of(W[t][v], o) for v in range(nv)]
    c1 = [lane_of(W[t][v], o + 1) for v in range(nv)]
    D = inv2(el(c0, 0), el(c1, 0), el(c0, 1), el(c1, 1))
    for j in range(0, 8 * nv, 2):
        l = o + j
        i00, n01, n10, i11 = D
        ar = ln == l
        ab = ar | (ln == l + 1)

        def rows_in(v, X, s0, s1):
            if j // 8 != v:
                return X
            return tuple(jnp.where(sb == j % 8, s0[k], jnp.where(sb == j % 8 + 1, s1[k], X[k])) for k in range(2))

        last = j + 2 == 8 * nv
        if not last:
            nxt, pivot = [], []
            for ahead in (l + 2, l + 3):
                d = [lane_of(W[t][v], ahead) for v in range(nv)]
                a, c = el(d, j), el(d, j + 1)
                s0 = csub(cmul(i00, a), cmul(n01, c))
                s1 = csub(cmul(i11, c), cmul(n10, a))
                for k in (j + 2, j + 3):
                    pivot.append(csub(el(d, k), cadd(cmul(el(c0, k), s0), cmul(el(c1, k), s1))))
                nxt.append(
                    [rows_in(v, csub(d[v], cadd(cmul(c0[v], s0), cmul(c1[v], s1))), s0, s1) for v in range(nv)]
                )
            D = inv2(pivot[0], pivot[2], pivot[1], pivot[3])
        new = []
        for s in range(2):
            r0 = rows_of(W[s][j // 8], j % 8)
            r1 = rows_of(W[s][(j + 1) // 8], (j + 1) % 8)
            if s == t:
                r0 = (jnp.where(ab, jnp.where(ar, 1.0, 0.0), r0[0]), jnp.where(ab, 0.0, r0[1]))
                r1 = (jnp.where(ab, jnp.where(ar, 0.0, 1.0), r1[0]), jnp.where(ab, 0.0, r1[1]))
            s0 = csub(cmul(i00, r0), cmul(n01, r1))
            s1 = csub(cmul(i11, r1), cmul(n10, r0))
            col = []
            for v in range(nv):
                X = W[s][v]
                if s == t:
                    X = (jnp.where(ab, 0.0, X[0]), jnp.where(ab, 0.0, X[1]))
                col.append(rows_in(v, csub(X, cadd(cmul(c0[v], s0), cmul(c1[v], s1))), s0, s1))
            new.append(col)
        W = new
        if not last:
            c0, c1 = nxt
    return W


def eliminate_rows_of_two(W, t, o, rows_of):
    nv = len(W[0])
    ln = lax.broadcasted_iota(jnp.int32, VREG, 1)
    sb = lax.broadcasted_iota(jnp.int32, VREG, 0)
    el = lambda c, j: rows_of(c[j // 8], j % 8)
    c0 = {0: lane_of(W[t][0], o)}
    c1 = {0: lane_of(W[t][0], o + 1)}
    D = inv2(el(c0, 0), el(c1, 0), el(c0, 1), el(c1, 1))
    for j in range(0, 8 * nv, 2):
        l = o + j
        c0 = [lane_of(W[t][v], l) for v in range(nv)]
        c1 = [lane_of(W[t][v], l + 1) for v in range(nv)]
        i00, n01, n10, i11 = D
        ar = ln == l
        ab = ar | (ln == l + 1)
        new = []
        for s in range(2):
            r0 = rows_of(W[s][j // 8], j % 8)
            r1 = rows_of(W[s][(j + 1) // 8], (j + 1) % 8)
            if s == t:
                r0 = (jnp.where(ab, jnp.where(ar, 1.0, 0.0), r0[0]), jnp.where(ab, 0.0, r0[1]))
                r1 = (jnp.where(ab, jnp.where(ar, 0.0, 1.0), r1[0]), jnp.where(ab, 0.0, r1[1]))
            s0 = csub(cmul(i00, r0), cmul(n01, r1))
            s1 = csub(cmul(i11, r1), cmul(n10, r0))
            col = []
            for v in range(nv):
                X = W[s][v]
                if s == t:
                    X = (jnp.where(ab, 0.0, X[0]), jnp.where(ab, 0.0, X[1]))
                X = csub(X, cadd(cmul(c0[v], s0), cmul(c1[v], s1)))
                if j // 8 == v:
                    X = tuple(
                        jnp.where(sb == j % 8, s0[k], jnp.where(sb == j % 8 + 1, s1[k], X[k])) for k in range(2)
                    )
                col.append(X)
            new.append(col)
        if j + 2 < 8 * nv:
            vs = sorted({j // 8, (j + 2) // 8})
            pivot = []
            for ahead in (l + 2, l + 3):
                d = {v: lane_of(W[t][v], ahead) for v in vs}
                a, c = el(d, j), el(d, j + 1)
                s0 = csub(cmul(i00, a), cmul(n01, c))
                s1 = csub(cmul(i11, c), cmul(n10, a))
                for k in (j + 2, j + 3):
                    pivot.append(csub(el(d, k), cadd(cmul(el(c0, k), s0), cmul(el(c1, k), s1))))
            D = inv2(pivot[0], pivot[2], pivot[1], pivot[3])
        W = new
    return W


def halves(x):
    high = x.astype(bf16)
    return high, (x - high.astype(f32)).astype(bf16)


def dot(a, b):
    return jnp.dot(a, b, preferred_element_type=f32)


def stacked(parts, axis):
    return jnp.concatenate(parts, axis)


def left_panel(M, o):
    ln = lax.broadcasted_iota(jnp.int32, M[0].shape, 1)
    here = (ln >= o) & (ln < o + SUB)
    both = jnp.where(here, M[0], 0.0) + pltpu.roll(jnp.where(here, M[1], 0.0), SUB, 1)
    high = both.astype(bf16).astype(f32)
    low = both - high
    return stacked([(high + pltpu.roll(low, 2 * SUB, 1)).astype(bf16), high.astype(bf16)], 1)


def right_panel(W, o):
    re = stacked([stacked([W[s][v][0] for v in range(4)], 0) for s in range(2)], 1)
    im = stacked([stacked([W[s][v][1] for v in range(4)], 0) for s in range(2)], 1)
    (rh, rl), (ih, il) = halves(re), halves(im)
    top_h, bottom_h = stacked([rh, ih], 1), stacked([-ih, rh], 1)
    top_l, bottom_l = stacked([rl, il], 1), stacked([-il, rl], 1)
    none = jnp.zeros((SUB, 2 * N), bf16)
    first = [top_h, bottom_h, top_h, bottom_h]
    second = [top_l, bottom_l, none, none]
    turn = o // SUB
    around = lambda x: [x[(g - turn) % 4] for g in range(4)]
    return stacked(around(first) + around(second), 0)


def invert(mats, rows_of, beside=None):
    def tile_steps(tile, carry):
        columns = [pl.ds(pl.multiple_of(128 * tile, 128), 128), pl.ds(pl.multiple_of(128 - 128 * tile, 128), 128)]
        rows_of.kept.clear()
        if beside is not None:
            beside(tile)
        eliminate = eliminate_rows if len(mats) == 1 else eliminate_rows_of_two

        def rows(q, height):
            return pl.ds(pl.multiple_of(128 * tile + SUB * q, SUB), height)

        panels = []
        for M in mats:
            whole = [[M[k][rows(0, SUB), c] for k in range(2)] for c in columns]
            panels.append([[tuple(x[8 * v : 8 * v + 8] for x in w) for v in range(4)] for w in whole])
        ln = lax.broadcasted_iota(jnp.int32, (N, 128), 1)
        for q in range(4):
            o = q * SUB
            here = (ln >= o) & (ln < o + SUB)
            lefts = [left_panel([M[k][:, columns[0]] for k in range(2)], o) for M in mats]
            strips = [left_panel([M[k][rows((q + 1) % 4, SUB), columns[0]] for k in range(2)], o) for M in mats]
            panels = [eliminate(W, 0, o, rows_of) for W in panels]
            following = []
            for M, L, W in zip(mats, lefts, panels):
                R = right_panel(W, o)
                if q < 3:
                    U = dot(strips.pop(0), R)
                    nxt = []
                    for s, c in enumerate(columns):
                        pairs = []
                        for k in range(2):
                            X = M[k][rows(q + 1, SUB), c]
                            if s == 0:
                                X = jnp.where(here[:SUB], 0.0, X)
                            pairs.append(X - U[:, k * N + s * 128 : k * N + s * 128 + 128])
                        nxt.append([tuple(x[8 * v : 8 * v + 8] for x in pairs) for v in range(4)])
                    following.append(nxt)
                U = dot(L, R)
                for s, c in enumerate(columns):
                    for k in range(2):
                        X = M[k][:, c]
                        if s == 0:
                            X = jnp.where(here, 0.0, X)
                        M[k][:, c] = X - U[:, k * N + s * 128 : k * N + s * 128 + 128]
                        M[k][rows(q, SUB), c] = stacked([W[s][v][k] for v in range(4)], 0)
            panels = following
        return carry

    lax.fori_loop(0, 2, tile_steps, 0)


def product(A, B):
    ah, al = halves(stacked([A[0], A[1]], 1))
    (rh, rl), (ih, il) = halves(B[0]), halves(B[1])
    bh = stacked([stacked([rh, ih], 1), stacked([-ih, rh], 1)], 0)
    bl = stacked([stacked([rl, il], 1), stacked([-il, rl], 1)], 0)
    C = dot(ah, bh) + (dot(ah, bl) + dot(al, bh))
    return C[:, :N], C[:, N:]


def planes(ref):
    return ref.at[0], ref.at[1]


def pair(ref):
    re, im = planes(ref)
    return re[...], im[...]


def put(ref, x):
    re, im = ref if isinstance(ref, tuple) else planes(ref)
    re[...], im[...] = x


def green_kernel(
    energy_ref, broadening_ref, contact_ref, offset_ref, weight_ref, herm_ref, hop_ref, out_ref, reach_ref,
    bank, work, scr,
):
    rows_of = Rows(scr)
    place = lax.axis_index("space")
    point, points = lax.axis_index("energy"), lax.axis_size("energy")
    side = place // 2
    e, eta, c = energy_ref[0], broadening_ref[0], contact_ref[0]

    even = lax.rem(point, 2) == 0
    reach = [-2, 2, -4, 4] + [jnp.where(even, a, b) for a, b in ((1, -1), (-1, -3), (3, 1), (-3, 3))]
    for k, d in enumerate(reach):
        inside = (point + d >= 0) & (point + d < points)
        total = jnp.float32(0.0)
        for j in range(8):
            total = total + jnp.where(inside & (offset_ref[0, j] == d), weight_ref[0, j], 0.0)
        reach_ref[k] = total

    row, column = triangles()
    eye = (row == column).astype(f32)

    def herm(k):
        mixed = herm_ref[k]
        turned = mixed.T
        return (
            jnp.where(row <= column, mixed, turned),
            jnp.where(row > column, mixed, jnp.where(row < column, -turned, 0.0)),
        )

    hop = lambda k: (hop_ref[k, 0], hop_ref[k, 1])
    back = lambda k: (hop_ref[k, 0].T, -hop_ref[k, 1].T)

    gram = product(hop(0), back(0))
    h0, h3 = herm(0), herm(3)
    put(planes(bank.at[0]), (e * eye - h0[0] - c * gram[1], eta * eye - h0[1] + c * gram[0]))
    put(planes(bank.at[1]), (e * eye - h3[0], (eta + c) * eye - h3[1]))
    put(planes(bank.at[2]), back(1))
    put(planes(bank.at[3]), hop(1))
    put(planes(bank.at[4]), hop(3))
    put(planes(bank.at[5]), back(3))

    @pl.when(side == 0)
    def _():
        put(planes(bank.at[6]), hop(2))
        put(planes(bank.at[7]), back(2))

    @pl.when(side == 1)
    def _():
        put(planes(bank.at[6]), back(2))
        put(planes(bank.at[7]), hop(2))

    invert([planes(bank.at[0]), planes(bank.at[1])], rows_of)

    def inner(i, sigma):
        h = herm(i)
        return (e * eye - h[0] - sigma[0], eta * eye - h[1] - sigma[1])

    far = 1 - side
    near_l, near_r = 2 + 2 * side, 3 + 2 * side
    right = product(pair(bank.at[far]), pair(bank.at[2 * far + 3]))
    put(work, inner(1 + far, product(pair(bank.at[2 * far + 2]), right)))

    def solve(step, carry):
        def near_product(tile):
            job = 2 * step + tile
            first = jnp.where(job == 0, side, near_l)
            second = jnp.where(job == 0, near_r, jnp.where(job == 1, 8, side))
            put(bank.at[jnp.where(job == 0, 8, jnp.where(job == 1, 9, 10))], product(pair(bank.at[first]), pair(bank.at[second])))

        invert([planes(work)], rows_of, near_product)

        @pl.when(step == 0)
        def _():
            right = product(pair(work), pair(bank.at[7]))
            middle = product(pair(bank.at[6]), right)
            put(work, inner(1 + side, cadd(pair(bank.at[9]), middle)))

        return carry

    lax.fori_loop(0, 2, solve, 0)

    @pl.when((place == 1) | (place == 2))
    def _():
        put(out_ref, pair(work))

    @pl.when((place == 0) | (place == 3))
    def _():
        put(out_ref, cadd(pair(bank.at[side]), product(pair(bank.at[8]), product(pair(work), pair(bank.at[10])))))


def green_block(energy, broadening, contact, offset, weight, herms, hops):
    vmem = pl.BlockSpec(memory_space=pltpu.VMEM)
    smem = pl.BlockSpec(memory_space=pltpu.SMEM)
    block = pltpu.VMEM((2, N, N), f32)
    return pl.pallas_call(
        green_kernel,
        out_shape=(jax.ShapeDtypeStruct((2, N, N), f32), jax.ShapeDtypeStruct((8,), f32)),
        in_specs=[smem] * 5 + [vmem] * 2,
        out_specs=(vmem, smem),
        scratch_shapes=[
            pltpu.VMEM((11, 2, N, N), f32),
            block,
            pltpu.VMEM((8 * SLOTS, 128), f32),
        ],
        compiler_params=pltpu.CompilerParams(vmem_limit_bytes=48 << 20),
        cost_estimate=pl.CostEstimate(flops=10**10, bytes_accessed=10**7, transcendentals=0),
    )(energy, broadening, contact, offset, weight, herms, hops)


def per_device(ham_blocks, hopping, energy, broadening, contact, phonon_offset, phonon_weight):
    herms, hops = gathered(ham_blocks[0], hopping[0])
    green, reach = green_block(energy, broadening, contact, phonon_offset, phonon_weight, herms, hops)
    total = phonon_sum(reach, green.reshape(512, N)).reshape(2, N, N)
    return (green[None, None], total[None, None])


def solution(mesh):
    placed = (
        P("space", None, None, None),
        P("space", None, None, None),
        P("energy"),
        P("energy"),
        P("energy"),
        P("energy", None),
        P("energy", None),
    )
    return jax.shard_map(
        per_device,
        mesh=mesh,
        in_specs=placed,
        out_specs=(P("energy", "space", None, None, None), P("energy", "space", None, None, None)),
        check_vma=False,
    )
```

```python
import functools

import jax
import jax.numpy as jnp
from jax import lax
from jax.experimental import pallas as pl
from jax.experimental.pallas import tpu as pltpu
from jax.sharding import PartitionSpec as P

N = 256
SUB = 32
f32 = jnp.float32
bf16 = jnp.bfloat16
VREG = (8, 128)
SLOTS = 256


CHUNKS = 8
PIECE = 512 // CHUNKS
MESH = pl.DeviceIdType.MESH


def greet(partners):
    barrier = pltpu.get_barrier_semaphore()
    for partner in partners:
        pl.semaphore_signal(barrier, inc=1, device_id=partner, device_id_type=MESH)
    pl.semaphore_wait(barrier, len(partners))


def triangles():
    row = lax.broadcasted_iota(jnp.int32, (N, N), 0)
    column = lax.broadcasted_iota(jnp.int32, (N, N), 1)
    return row, column


def gather_kernel(ham_ref, hop_ref, herms_ref, hops_ref, ham, herm, local_sem, send_sem, recv_sem):
    places = lax.axis_size("space")
    me = lax.axis_index("space")
    point = lax.axis_index("energy")
    core = lax.rem(point, 2)
    up, down = lax.rem(me + 1, places), lax.rem(me + places - 1, places)
    across = lax.rem(me + 2, places)
    above, below, beside = {"space": up}, {"space": down}, {"energy": point + 1 - 2 * core}
    fetch = pltpu.make_async_copy(ham_ref, ham, local_sem.at[0])
    fetch.start()
    own = [pltpu.make_async_copy(hop_ref, hops_ref.at[me], local_sem.at[1])]
    own[0].start()
    greet((above, below, beside))
    rows = pl.ds(pl.multiple_of(128 * core, 128), 128)
    started = []
    herms_of = lambda k: herms_ref.at[k, rows]
    hops_of = lambda k, i: hops_ref.at[k, i, rows]

    def send(source, target, to, slot):
        copy = pltpu.make_async_remote_copy(
            src_ref=source,
            dst_ref=target,
            send_sem=send_sem.at[slot],
            recv_sem=recv_sem.at[slot],
            device_id=to,
            device_id_type=MESH,
        )
        copy.start()
        started.append(copy)
        return copy

    hop_up = [send(hop_ref.at[i, rows], hops_of(me, i), above, i) for i in (0, 1)]
    hop_down = [send(hop_ref.at[i, rows], hops_of(me, i), below, 2 + i) for i in (1, 0)][::-1]
    fetch.wait()
    row, column = triangles()
    herm[...] = 0.5 * jnp.where(row <= column, ham[0] + ham[0].T, ham[1] - ham[1].T)
    herm_up = send(herm.at[rows], herms_of(me), above, 4)
    herm_down = send(herm.at[rows], herms_of(me), below, 5)
    own.append(pltpu.make_async_copy(herm, herms_ref.at[me], local_sem.at[2]))
    own[1].start()
    hop_up[0].wait_recv()
    far_up = send(hops_of(down, 0), hops_of(down, 0), above, 6)
    swaps = [send(hops_of(down, 0), hops_of(down, 0), beside, 9)]
    hop_down[1].wait_recv()
    far_down = send(hops_of(up, 1), hops_of(up, 1), below, 7)
    swaps.append(send(hops_of(up, 1), hops_of(up, 1), beside, 10))
    hop_up[1].wait_recv()
    swaps.append(send(hops_of(down, 1), hops_of(down, 1), beside, 11))
    hop_down[0].wait_recv()
    swaps.append(send(hops_of(up, 0), hops_of(up, 0), beside, 12))
    half = 64
    top = pl.ds(pl.multiple_of(128 * core, 64), half)
    bottom = pl.ds(pl.multiple_of(128 * core + half, 64), half)
    herm_up.wait_recv()
    far_top = send(herms_ref.at[down, top], herms_ref.at[down, top], above, 8)
    swaps.append(send(herms_of(down), herms_of(down), beside, 13))
    herm_down.wait_recv()
    far_bottom = send(herms_ref.at[up, bottom], herms_ref.at[up, bottom], below, 14)
    swaps.append(send(herms_of(up), herms_of(up), beside, 15))
    far_up.wait_recv()
    swaps.append(send(hops_of(across, 0), hops_of(across, 0), beside, 16))
    far_down.wait_recv()
    swaps.append(send(hops_of(across, 1), hops_of(across, 1), beside, 17))
    far_top.wait_recv()
    swaps.append(send(herms_ref.at[across, top], herms_ref.at[across, top], beside, 18))
    far_bottom.wait_recv()
    swaps.append(send(herms_ref.at[across, bottom], herms_ref.at[across, bottom], beside, 19))
    for copy in swaps:
        copy.wait_recv()
    for copy in started:
        copy.wait_send()
    for copy in own:
        copy.wait()


def gathered(ham, hop):
    anywhere = pl.BlockSpec(memory_space=pl.ANY)
    return pl.pallas_call(
        gather_kernel,
        out_shape=(jax.ShapeDtypeStruct((4, N, N), f32), jax.ShapeDtypeStruct((4, 2, N, N), f32)),
        in_specs=[pl.BlockSpec(memory_space=pltpu.HBM)] * 2,
        out_specs=(anywhere, anywhere),
        scratch_shapes=[
            pltpu.VMEM((2, N, N), f32),
            pltpu.VMEM((N, N), f32),
            pltpu.SemaphoreType.DMA((3,)),
            pltpu.SemaphoreType.DMA((20,)),
            pltpu.SemaphoreType.DMA((20,)),
        ],
        compiler_params=pltpu.CompilerParams(collective_id=0, has_side_effects=True, vmem_limit_bytes=16 << 20),
        cost_estimate=pl.CostEstimate(flops=10**6, bytes_accessed=10**7, transcendentals=0),
    )(ham, hop)


def phonon_kernel(weight_ref, green_ref, out_ref, near, far, side, send_sem, recv_sem):
    points = lax.axis_size("energy")
    point = lax.axis_index("energy")
    core = lax.rem(point, 2)
    after, before = {"energy": lax.rem(point + 2, points)}, {"energy": lax.rem(point + points - 2, points)}
    beside = {"energy": point + 1 - 2 * core}
    along = (after, before)
    started = []

    def piece(i):
        return pl.ds(PIECE * i, PIECE)

    def send(source, target, to, slot):
        copy = pltpu.make_async_remote_copy(
            src_ref=source,
            dst_ref=target,
            send_sem=send_sem.at[slot],
            recv_sem=recv_sem.at[slot],
            device_id=to,
            device_id_type=MESH,
        )
        copy.start()
        started.append(copy)
        return copy

    def add(i, terms):
        total = out_ref[piece(i)]
        for k, ref in terms:
            total = total + weight_ref[k] * ref[piece(i)]
        out_ref[piece(i)] = total

    chip, chips = point // 2, points // 2
    sends = (chip < chips - 1, chip > 0)
    gets = (chip > 0, chip < chips - 1)
    relays = (sends[0] & gets[0], sends[1] & gets[1])
    gets_far = (chip > 1, chip < chips - 2)
    for d in range(2):
        for ref, reached in ((near, gets[d]), (far, gets_far[d])):

            @pl.when(jnp.logical_not(reached))
            def _():
                ref[d] = jnp.zeros_like(ref[d])

    greet((after, before, beside))
    first, second, swap = {}, {}, {}
    waits = []

    def send_if(condition, source, target, to, slot):
        copy = pltpu.make_async_remote_copy(
            src_ref=source,
            dst_ref=target,
            send_sem=send_sem.at[slot],
            recv_sem=recv_sem.at[slot],
            device_id=to,
            device_id_type=MESH,
        )
        pl.when(condition)(copy.start)
        waits.append((condition, copy))
        return copy

    for i in range(CHUNKS):
        for d in range(2):
            first[d, i] = send_if(sends[d], green_ref.at[piece(i)], near.at[d, piece(i)], along[d], d * CHUNKS + i)
    for i in range(CHUNKS):
        swap[0, i] = send(green_ref.at[piece(i)], side.at[0, piece(i)], beside, 4 * CHUNKS + i)
    for i in range(CHUNKS):
        for d in range(2):
            pl.when(gets[d])(first[d, i].wait_recv)
            second[d, i] = send_if(
                relays[d], near.at[d, piece(i)], far.at[d, piece(i)], along[d], (2 + d) * CHUNKS + i
            )
            swap[1 + d, i] = send(near.at[d, piece(i)], side.at[1 + d, piece(i)], beside, (5 + d) * CHUNKS + i)
        swap[0, i].wait_recv()
        out_ref[piece(i)] = weight_ref[4] * side[0, piece(i)]
        add(i, [(0, near.at[0]), (1, near.at[1])])
    for i in range(CHUNKS):
        for d in range(2):
            pl.when(gets_far[d])(second[d, i].wait_recv)
        swap[3, i] = send(far.at[1 - core, piece(i)], side.at[3, piece(i)], beside, 7 * CHUNKS + i)
        swap[1, i].wait_recv()
        swap[2, i].wait_recv()
        add(i, [(2, far.at[0]), (3, far.at[1]), (5, side.at[1]), (6, side.at[2])])
    for i in range(CHUNKS):
        swap[3, i].wait_recv()
        add(i, [(7, side.at[3])])
    for copy in started:
        copy.wait_send()
    for condition, copy in waits:
        pl.when(condition)(copy.wait_send)


def phonon_sum(weights, green):
    vmem = pl.BlockSpec(memory_space=pltpu.VMEM)
    block = (512, N)
    return pl.pallas_call(
        phonon_kernel,
        out_shape=jax.ShapeDtypeStruct(block, f32),
        in_specs=[pl.BlockSpec(memory_space=pltpu.SMEM), pl.BlockSpec(memory_space=pl.ANY)],
        out_specs=vmem,
        scratch_shapes=[
            pltpu.VMEM((2, *block), f32),
            pltpu.VMEM((2, *block), f32),
            pltpu.VMEM((4, *block), f32),
            pltpu.SemaphoreType.DMA((8 * CHUNKS,)),
            pltpu.SemaphoreType.DMA((8 * CHUNKS,)),
        ],
        compiler_params=pltpu.CompilerParams(collective_id=1, has_side_effects=True, vmem_limit_bytes=24 << 20),
        cost_estimate=pl.CostEstimate(flops=10**6, bytes_accessed=10**7, transcendentals=0),
    )(weights, green)


def cmul(a, b):
    return (a[0] * b[0] - a[1] * b[1], a[0] * b[1] + a[1] * b[0])


def csub(a, b):
    return (a[0] - b[0], a[1] - b[1])


def cadd(a, b):
    return (a[0] + b[0], a[1] + b[1])


def lane_of(x, l):
    return tuple(jnp.broadcast_to(a[:, l : l + 1], VREG) for a in x)


def inv2(p00, p01, p10, p11):
    det = csub(cmul(p00, p11), cmul(p01, p10))
    d = 1.0 / (det[0] * det[0] + det[1] * det[1])
    q = (det[0] * d, -det[1] * d)
    return cmul(p11, q), cmul(p01, q), cmul(p10, q), cmul(p00, q)


class Rows:
    def __init__(self, ref):
        self.ref, self.next, self.kept = ref, 0, {}

    def __call__(self, x, j):
        out = []
        for a in x:
            if id(a) not in self.kept:
                slot = self.next
                self.next = (slot + 1) % SLOTS
                self.ref[slot * 8 : slot * 8 + 8, :] = a
                self.kept[id(a)] = (slot, a)
            slot = self.kept[id(a)][0]
            out.append(self.ref[pl.ds(slot * 8 + j, 8, stride=0), :])
        return tuple(out)


def eliminate_rows(W, t, o, rows_of):
    nv = len(W[0])
    ln = lax.broadcasted_iota(jnp.int32, VREG, 1)
    sb = lax.broadcasted_iota(jnp.int32, VREG, 0)
    el = lambda c, j: rows_of(c[j // 8], j % 8)
    c0 = [lane_of(W[t][v], o) for v in range(nv)]
    c1 = [lane_of(W[t][v], o + 1) for v in range(nv)]
    D = inv2(el(c0, 0), el(c1, 0), el(c0, 1), el(c1, 1))
    for j in range(0, 8 * nv, 2):
        l = o + j
        i00, n01, n10, i11 = D
        ar = ln == l
        ab = ar | (ln == l + 1)

        def rows_in(v, X, s0, s1):
            if j // 8 != v:
                return X
            return tuple(jnp.where(sb == j % 8, s0[k], jnp.where(sb == j % 8 + 1, s1[k], X[k])) for k in range(2))

        last = j + 2 == 8 * nv
        if not last:
            nxt, pivot = [], []
            for ahead in (l + 2, l + 3):
                d = [lane_of(W[t][v], ahead) for v in range(nv)]
                a, c = el(d, j), el(d, j + 1)
                s0 = csub(cmul(i00, a), cmul(n01, c))
                s1 = csub(cmul(i11, c), cmul(n10, a))
                for k in (j + 2, j + 3):
                    pivot.append(csub(el(d, k), cadd(cmul(el(c0, k), s0), cmul(el(c1, k), s1))))
                nxt.append(
                    [rows_in(v, csub(d[v], cadd(cmul(c0[v], s0), cmul(c1[v], s1))), s0, s1) for v in range(nv)]
                )
            D = inv2(pivot[0], pivot[2], pivot[1], pivot[3])
        new = []
        for s in range(2):
            r0 = rows_of(W[s][j // 8], j % 8)
            r1 = rows_of(W[s][(j + 1) // 8], (j + 1) % 8)
            if s == t:
                r0 = (jnp.where(ab, jnp.where(ar, 1.0, 0.0), r0[0]), jnp.where(ab, 0.0, r0[1]))
                r1 = (jnp.where(ab, jnp.where(ar, 0.0, 1.0), r1[0]), jnp.where(ab, 0.0, r1[1]))
            s0 = csub(cmul(i00, r0), cmul(n01, r1))
            s1 = csub(cmul(i11, r1), cmul(n10, r0))
            col = []
            for v in range(nv):
                X = W[s][v]
                if s == t:
                    X = (jnp.where(ab, 0.0, X[0]), jnp.where(ab, 0.0, X[1]))
                col.append(rows_in(v, csub(X, cadd(cmul(c0[v], s0), cmul(c1[v], s1))), s0, s1))
            new.append(col)
        W = new
        if not last:
            c0, c1 = nxt
    return W


def eliminate_rows_of_two(W, t, o, rows_of):
    nv = len(W[0])
    ln = lax.broadcasted_iota(jnp.int32, VREG, 1)
    sb = lax.broadcasted_iota(jnp.int32, VREG, 0)
    el = lambda c, j: rows_of(c[j // 8], j % 8)
    c0 = {0: lane_of(W[t][0], o)}
    c1 = {0: lane_of(W[t][0], o + 1)}
    D = inv2(el(c0, 0), el(c1, 0), el(c0, 1), el(c1, 1))
    for j in range(0, 8 * nv, 2):
        l = o + j
        c0 = [lane_of(W[t][v], l) for v in range(nv)]
        c1 = [lane_of(W[t][v], l + 1) for v in range(nv)]
        i00, n01, n10, i11 = D
        ar = ln == l
        ab = ar | (ln == l + 1)
        new = []
        for s in range(2):
            r0 = rows_of(W[s][j // 8], j % 8)
            r1 = rows_of(W[s][(j + 1) // 8], (j + 1) % 8)
            if s == t:
                r0 = (jnp.where(ab, jnp.where(ar, 1.0, 0.0), r0[0]), jnp.where(ab, 0.0, r0[1]))
                r1 = (jnp.where(ab, jnp.where(ar, 0.0, 1.0), r1[0]), jnp.where(ab, 0.0, r1[1]))
            s0 = csub(cmul(i00, r0), cmul(n01, r1))
            s1 = csub(cmul(i11, r1), cmul(n10, r0))
            col = []
            for v in range(nv):
                X = W[s][v]
                if s == t:
                    X = (jnp.where(ab, 0.0, X[0]), jnp.where(ab, 0.0, X[1]))
                X = csub(X, cadd(cmul(c0[v], s0), cmul(c1[v], s1)))
                if j // 8 == v:
                    X = tuple(
                        jnp.where(sb == j % 8, s0[k], jnp.where(sb == j % 8 + 1, s1[k], X[k])) for k in range(2)
                    )
                col.append(X)
            new.append(col)
        if j + 2 < 8 * nv:
            vs = sorted({j // 8, (j + 2) // 8})
            pivot = []
            for ahead in (l + 2, l + 3):
                d = {v: lane_of(W[t][v], ahead) for v in vs}
                a, c = el(d, j), el(d, j + 1)
                s0 = csub(cmul(i00, a), cmul(n01, c))
                s1 = csub(cmul(i11, c), cmul(n10, a))
                for k in (j + 2, j + 3):
                    pivot.append(csub(el(d, k), cadd(cmul(el(c0, k), s0), cmul(el(c1, k), s1))))
            D = inv2(pivot[0], pivot[2], pivot[1], pivot[3])
        W = new
    return W


def halves(x):
    high = x.astype(bf16)
    return high, (x - high.astype(f32)).astype(bf16)


def dot(a, b):
    return jnp.dot(a, b, preferred_element_type=f32)


def stacked(parts, axis):
    return jnp.concatenate(parts, axis)


def left_panel(M, o):
    ln = lax.broadcasted_iota(jnp.int32, M[0].shape, 1)
    here = (ln >= o) & (ln < o + SUB)
    both = jnp.where(here, M[0], 0.0) + pltpu.roll(jnp.where(here, M[1], 0.0), SUB, 1)
    high = both.astype(bf16).astype(f32)
    low = both - high
    return stacked([(high + pltpu.roll(low, 2 * SUB, 1)).astype(bf16), high.astype(bf16)], 1)


def right_panel(W, o):
    re = stacked([stacked([W[s][v][0] for v in range(4)], 0) for s in range(2)], 1)
    im = stacked([stacked([W[s][v][1] for v in range(4)], 0) for s in range(2)], 1)
    (rh, rl), (ih, il) = halves(re), halves(im)
    top_h, bottom_h = stacked([rh, ih], 1), stacked([-ih, rh], 1)
    top_l, bottom_l = stacked([rl, il], 1), stacked([-il, rl], 1)
    none = jnp.zeros((SUB, 2 * N), bf16)
    first = [top_h, bottom_h, top_h, bottom_h]
    second = [top_l, bottom_l, none, none]
    turn = o // SUB
    around = lambda x: [x[(g - turn) % 4] for g in range(4)]
    return stacked(around(first) + around(second), 0)


def invert(mats, rows_of, beside=None):
    def tile_steps(tile, carry):
        columns = [pl.ds(pl.multiple_of(128 * tile, 128), 128), pl.ds(pl.multiple_of(128 - 128 * tile, 128), 128)]
        rows_of.kept.clear()
        if beside is not None:
            beside(tile)
        eliminate = eliminate_rows if len(mats) == 1 else eliminate_rows_of_two

        def rows(q, height):
            return pl.ds(pl.multiple_of(128 * tile + SUB * q, SUB), height)

        panels = []
        for M in mats:
            whole = [[M[k][rows(0, SUB), c] for k in range(2)] for c in columns]
            panels.append([[tuple(x[8 * v : 8 * v + 8] for x in w) for v in range(4)] for w in whole])
        ln = lax.broadcasted_iota(jnp.int32, (N, 128), 1)
        for q in range(4):
            o = q * SUB
            here = (ln >= o) & (ln < o + SUB)
            lefts = [left_panel([M[k][:, columns[0]] for k in range(2)], o) for M in mats]
            strips = [left_panel([M[k][rows((q + 1) % 4, SUB), columns[0]] for k in range(2)], o) for M in mats]
            panels = [eliminate(W, 0, o, rows_of) for W in panels]
            following = []
            for M, L, W in zip(mats, lefts, panels):
                R = right_panel(W, o)
                if q < 3:
                    U = dot(strips.pop(0), R)
                    nxt = []
                    for s, c in enumerate(columns):
                        pairs = []
                        for k in range(2):
                            X = M[k][rows(q + 1, SUB), c]
                            if s == 0:
                                X = jnp.where(here[:SUB], 0.0, X)
                            pairs.append(X - U[:, k * N + s * 128 : k * N + s * 128 + 128])
                        nxt.append([tuple(x[8 * v : 8 * v + 8] for x in pairs) for v in range(4)])
                    following.append(nxt)
                U = dot(L, R)
                for s, c in enumerate(columns):
                    for k in range(2):
                        X = M[k][:, c]
                        if s == 0:
                            X = jnp.where(here, 0.0, X)
                        M[k][:, c] = X - U[:, k * N + s * 128 : k * N + s * 128 + 128]
                        M[k][rows(q, SUB), c] = stacked([W[s][v][k] for v in range(4)], 0)
            panels = following
        return carry

    lax.fori_loop(0, 2, tile_steps, 0)


def product(A, B):
    ah, al = halves(stacked([A[0], A[1]], 1))
    (rh, rl), (ih, il) = halves(B[0]), halves(B[1])
    bh = stacked([stacked([rh, ih], 1), stacked([-ih, rh], 1)], 0)
    bl = stacked([stacked([rl, il], 1), stacked([-il, rl], 1)], 0)
    C = dot(ah, bh) + (dot(ah, bl) + dot(al, bh))
    return C[:, :N], C[:, N:]


def planes(ref):
    return ref.at[0], ref.at[1]


def pair(ref):
    re, im = planes(ref)
    return re[...], im[...]


def put(ref, x):
    re, im = ref if isinstance(ref, tuple) else planes(ref)
    re[...], im[...] = x


def green_kernel(
    energy_ref, broadening_ref, contact_ref, offset_ref, weight_ref, herm_ref, hop_ref, out_ref, reach_ref, kept_ref,
    bank, work, scr,
):
    rows_of = Rows(scr)
    place = lax.axis_index("space")
    point, points = lax.axis_index("energy"), lax.axis_size("energy")
    side = place // 2
    e, eta, c = energy_ref[0], broadening_ref[0], contact_ref[0]

    even = lax.rem(point, 2) == 0
    reach = [-2, 2, -4, 4] + [jnp.where(even, a, b) for a, b in ((1, -1), (-1, -3), (3, 1), (-3, 3))]
    for k, d in enumerate(reach):
        inside = (point + d >= 0) & (point + d < points)
        total = jnp.float32(0.0)
        for j in range(8):
            total = total + jnp.where(inside & (offset_ref[0, j] == d), weight_ref[0, j], 0.0)
        reach_ref[k] = total

    row, column = triangles()
    eye = (row == column).astype(f32)

    def herm(k):
        mixed = herm_ref[k]
        turned = mixed.T
        return (
            jnp.where(row <= column, mixed, turned),
            jnp.where(row > column, mixed, jnp.where(row < column, -turned, 0.0)),
        )

    hop = lambda k: (hop_ref[k, 0], hop_ref[k, 1])
    back = lambda k: (hop_ref[k, 0].T, -hop_ref[k, 1].T)

    gram = product(hop(0), back(0))
    h0, h3 = herm(0), herm(3)
    put(planes(bank.at[0]), (e * eye - h0[0] - c * gram[1], eta * eye - h0[1] + c * gram[0]))
    put(planes(bank.at[1]), (e * eye - h3[0], (eta + c) * eye - h3[1]))
    put(planes(bank.at[2]), back(1))
    put(planes(bank.at[3]), hop(1))
    put(planes(bank.at[4]), hop(3))
    put(planes(bank.at[5]), back(3))

    @pl.when(side == 0)
    def _():
        put(planes(bank.at[6]), hop(2))
        put(planes(bank.at[7]), back(2))

    @pl.when(side == 1)
    def _():
        put(planes(bank.at[6]), back(2))
        put(planes(bank.at[7]), hop(2))

    invert([planes(bank.at[0]), planes(bank.at[1])], rows_of)

    def inner(i, sigma):
        h = herm(i)
        return (e * eye - h[0] - sigma[0], eta * eye - h[1] - sigma[1])

    far = 1 - side
    near_l, near_r = 2 + 2 * side, 3 + 2 * side
    right = product(pair(bank.at[far]), pair(bank.at[2 * far + 3]))
    put(work, inner(1 + far, product(pair(bank.at[2 * far + 2]), right)))

    def solve(step, carry):
        def near_product(tile):
            job = 2 * step + tile
            first = jnp.where(job == 0, side, near_l)
            second = jnp.where(job == 0, near_r, jnp.where(job == 1, 8, side))
            put(bank.at[jnp.where(job == 0, 8, jnp.where(job == 1, 9, 10))], product(pair(bank.at[first]), pair(bank.at[second])))

        invert([planes(work)], rows_of, near_product)

        @pl.when(step == 0)
        def _():
            right = product(pair(work), pair(bank.at[7]))
            middle = product(pair(bank.at[6]), right)
            put(work, inner(1 + side, cadd(pair(bank.at[9]), middle)))

        return carry

    lax.fori_loop(0, 2, solve, 0)

    def finish(x):
        put(out_ref, x)
        put(kept_ref, x)

    @pl.when((place == 1) | (place == 2))
    def _():
        finish(pair(work))

    @pl.when((place == 0) | (place == 3))
    def _():
        finish(cadd(pair(bank.at[side]), product(pair(bank.at[8]), product(pair(work), pair(bank.at[10])))))


def green_block(energy, broadening, contact, offset, weight, herms, hops):
    vmem = pl.BlockSpec(memory_space=pltpu.VMEM)
    smem = pl.BlockSpec(memory_space=pltpu.SMEM)
    block = pltpu.VMEM((2, N, N), f32)
    return pl.pallas_call(
        green_kernel,
        out_shape=(
            jax.ShapeDtypeStruct((2, N, N), f32),
            jax.ShapeDtypeStruct((8,), f32),
            jax.ShapeDtypeStruct((2, N, N), f32),
        ),
        in_specs=[smem] * 5 + [vmem] * 2,
        out_specs=(vmem, smem, vmem),
        scratch_shapes=[
            pltpu.VMEM((11, 2, N, N), f32),
            block,
            pltpu.VMEM((8 * SLOTS, 128), f32),
        ],
        compiler_params=pltpu.CompilerParams(vmem_limit_bytes=48 << 20),
        cost_estimate=pl.CostEstimate(flops=10**10, bytes_accessed=10**7, transcendentals=0),
    )(energy, broadening, contact, offset, weight, herms, hops)


def per_device(ham_blocks, hopping, energy, broadening, contact, phonon_offset, phonon_weight):
    herms, hops = gathered(ham_blocks[0], hopping[0])
    green, reach, kept = green_block(energy, broadening, contact, phonon_offset, phonon_weight, herms, hops)
    total = phonon_sum(reach, kept.reshape(512, N)).reshape(2, N, N)
    return (green[None, None], total[None, None])


def solution(mesh):
    placed = (
        P("space", None, None, None),
        P("space", None, None, None),
        P("energy"),
        P("energy"),
        P("energy"),
        P("energy", None),
        P("energy", None),
    )
    return jax.shard_map(
        per_device,
        mesh=mesh,
        in_specs=placed,
        out_specs=(P("energy", "space", None, None, None), P("energy", "space", None, None, None)),
        check_vma=False,
    )
```

```python
import functools

import jax
import jax.numpy as jnp
from jax import lax
from jax.experimental import pallas as pl
from jax.experimental.pallas import tpu as pltpu
from jax.sharding import PartitionSpec as P

N = 256
SUB = 32
f32 = jnp.float32
bf16 = jnp.bfloat16
VREG = (8, 128)
SLOTS = 256


CHUNKS = 4
PIECE = 512 // CHUNKS
MESH = pl.DeviceIdType.MESH


def greet(partners):
    barrier = pltpu.get_barrier_semaphore()
    for partner in partners:
        pl.semaphore_signal(barrier, inc=1, device_id=partner, device_id_type=MESH)
    pl.semaphore_wait(barrier, len(partners))


def triangles():
    row = lax.broadcasted_iota(jnp.int32, (N, N), 0)
    column = lax.broadcasted_iota(jnp.int32, (N, N), 1)
    return row, column


def gather_kernel(ham_ref, hop_ref, herms_ref, hops_ref, ham, herm, local_sem, send_sem, recv_sem):
    places = lax.axis_size("space")
    me = lax.axis_index("space")
    point = lax.axis_index("energy")
    core = lax.rem(point, 2)
    up, down = lax.rem(me + 1, places), lax.rem(me + places - 1, places)
    across = lax.rem(me + 2, places)
    above, below, beside = {"space": up}, {"space": down}, {"energy": point + 1 - 2 * core}
    fetch = pltpu.make_async_copy(ham_ref, ham, local_sem.at[0])
    fetch.start()
    own = [pltpu.make_async_copy(hop_ref, hops_ref.at[me], local_sem.at[1])]
    own[0].start()
    greet((above, below, beside))
    rows = pl.ds(pl.multiple_of(128 * core, 128), 128)
    started = []
    herms_of = lambda k: herms_ref.at[k, rows]
    hops_of = lambda k, i: hops_ref.at[k, i, rows]

    def send(source, target, to, slot):
        copy = pltpu.make_async_remote_copy(
            src_ref=source,
            dst_ref=target,
            send_sem=send_sem.at[slot],
            recv_sem=recv_sem.at[slot],
            device_id=to,
            device_id_type=MESH,
        )
        copy.start()
        started.append(copy)
        return copy

    hop_up = [send(hop_ref.at[i, rows], hops_of(me, i), above, i) for i in (0, 1)]
    hop_down = [send(hop_ref.at[i, rows], hops_of(me, i), below, 2 + i) for i in (1, 0)][::-1]
    fetch.wait()
    row, column = triangles()
    herm[...] = 0.5 * jnp.where(row <= column, ham[0] + ham[0].T, ham[1] - ham[1].T)
    herm_up = send(herm.at[rows], herms_of(me), above, 4)
    herm_down = send(herm.at[rows], herms_of(me), below, 5)
    own.append(pltpu.make_async_copy(herm, herms_ref.at[me], local_sem.at[2]))
    own[1].start()
    hop_up[0].wait_recv()
    far_up = send(hops_of(down, 0), hops_of(down, 0), above, 6)
    swaps = [send(hops_of(down, 0), hops_of(down, 0), beside, 9)]
    hop_down[1].wait_recv()
    far_down = send(hops_of(up, 1), hops_of(up, 1), below, 7)
    swaps.append(send(hops_of(up, 1), hops_of(up, 1), beside, 10))
    hop_up[1].wait_recv()
    swaps.append(send(hops_of(down, 1), hops_of(down, 1), beside, 11))
    hop_down[0].wait_recv()
    swaps.append(send(hops_of(up, 0), hops_of(up, 0), beside, 12))
    half = 64
    top = pl.ds(pl.multiple_of(128 * core, 64), half)
    bottom = pl.ds(pl.multiple_of(128 * core + half, 64), half)
    herm_up.wait_recv()
    far_top = send(herms_ref.at[down, top], herms_ref.at[down, top], above, 8)
    swaps.append(send(herms_of(down), herms_of(down), beside, 13))
    herm_down.wait_recv()
    far_bottom = send(herms_ref.at[up, bottom], herms_ref.at[up, bottom], below, 14)
    swaps.append(send(herms_of(up), herms_of(up), beside, 15))
    far_up.wait_recv()
    swaps.append(send(hops_of(across, 0), hops_of(across, 0), beside, 16))
    far_down.wait_recv()
    swaps.append(send(hops_of(across, 1), hops_of(across, 1), beside, 17))
    far_top.wait_recv()
    swaps.append(send(herms_ref.at[across, top], herms_ref.at[across, top], beside, 18))
    far_bottom.wait_recv()
    swaps.append(send(herms_ref.at[across, bottom], herms_ref.at[across, bottom], beside, 19))
    for copy in swaps:
        copy.wait_recv()
    for copy in started:
        copy.wait_send()
    for copy in own:
        copy.wait()


def gathered(ham, hop):
    anywhere = pl.BlockSpec(memory_space=pl.ANY)
    return pl.pallas_call(
        gather_kernel,
        out_shape=(jax.ShapeDtypeStruct((4, N, N), f32), jax.ShapeDtypeStruct((4, 2, N, N), f32)),
        in_specs=[pl.BlockSpec(memory_space=pltpu.HBM)] * 2,
        out_specs=(anywhere, anywhere),
        scratch_shapes=[
            pltpu.VMEM((2, N, N), f32),
            pltpu.VMEM((N, N), f32),
            pltpu.SemaphoreType.DMA((3,)),
            pltpu.SemaphoreType.DMA((20,)),
            pltpu.SemaphoreType.DMA((20,)),
        ],
        compiler_params=pltpu.CompilerParams(collective_id=0, has_side_effects=True, vmem_limit_bytes=16 << 20),
        cost_estimate=pl.CostEstimate(flops=10**6, bytes_accessed=10**7, transcendentals=0),
    )(ham, hop)


def phonon_kernel(weight_ref, green_ref, out_ref, near, far, side, send_sem, recv_sem):
    points = lax.axis_size("energy")
    point = lax.axis_index("energy")
    core = lax.rem(point, 2)
    after, before = {"energy": lax.rem(point + 2, points)}, {"energy": lax.rem(point + points - 2, points)}
    beside = {"energy": point + 1 - 2 * core}
    along = (after, before)
    started = []

    def piece(i):
        return pl.ds(PIECE * i, PIECE)

    def send(source, target, to, slot):
        copy = pltpu.make_async_remote_copy(
            src_ref=source,
            dst_ref=target,
            send_sem=send_sem.at[slot],
            recv_sem=recv_sem.at[slot],
            device_id=to,
            device_id_type=MESH,
        )
        copy.start()
        started.append(copy)
        return copy

    def add(i, terms):
        total = out_ref[piece(i)]
        for k, ref in terms:
            total = total + weight_ref[k] * ref[piece(i)]
        out_ref[piece(i)] = total

    chip, chips = point // 2, points // 2
    sends = (chip < chips - 1, chip > 0)
    gets = (chip > 0, chip < chips - 1)
    relays = (sends[0] & gets[0], sends[1] & gets[1])
    gets_far = (chip > 1, chip < chips - 2)
    for d in range(2):
        for ref, reached in ((near, gets[d]), (far, gets_far[d])):

            @pl.when(jnp.logical_not(reached))
            def _():
                ref[d] = jnp.zeros_like(ref[d])

    greet((after, before, beside))
    first, second, swap = {}, {}, {}
    waits = []

    def send_if(condition, source, target, to, slot):
        copy = pltpu.make_async_remote_copy(
            src_ref=source,
            dst_ref=target,
            send_sem=send_sem.at[slot],
            recv_sem=recv_sem.at[slot],
            device_id=to,
            device_id_type=MESH,
        )
        pl.when(condition)(copy.start)
        waits.append((condition, copy))
        return copy

    for i in range(CHUNKS):
        for d in range(2):
            first[d, i] = send_if(sends[d], green_ref.at[piece(i)], near.at[d, piece(i)], along[d], d * CHUNKS + i)
    for i in range(CHUNKS):
        swap[0, i] = send(green_ref.at[piece(i)], side.at[0, piece(i)], beside, 4 * CHUNKS + i)
    for i in range(CHUNKS):
        for d in range(2):
            pl.when(gets[d])(first[d, i].wait_recv)
            second[d, i] = send_if(
                relays[d], near.at[d, piece(i)], far.at[d, piece(i)], along[d], (2 + d) * CHUNKS + i
            )
            swap[1 + d, i] = send(near.at[d, piece(i)], side.at[1 + d, piece(i)], beside, (5 + d) * CHUNKS + i)
        swap[0, i].wait_recv()
        out_ref[piece(i)] = weight_ref[4] * side[0, piece(i)]
        add(i, [(0, near.at[0]), (1, near.at[1])])
    for i in range(CHUNKS):
        for d in range(2):
            pl.when(gets_far[d])(second[d, i].wait_recv)
        swap[3, i] = send(far.at[1 - core, piece(i)], side.at[3, piece(i)], beside, 7 * CHUNKS + i)
        swap[1, i].wait_recv()
        swap[2, i].wait_recv()
        add(i, [(2, far.at[0]), (3, far.at[1]), (5, side.at[1]), (6, side.at[2])])
    for i in range(CHUNKS):
        swap[3, i].wait_recv()
        add(i, [(7, side.at[3])])
    for copy in started:
        copy.wait_send()
    for condition, copy in waits:
        pl.when(condition)(copy.wait_send)


def phonon_sum(weights, green):
    vmem = pl.BlockSpec(memory_space=pltpu.VMEM)
    block = (512, N)
    return pl.pallas_call(
        phonon_kernel,
        out_shape=jax.ShapeDtypeStruct(block, f32),
        in_specs=[pl.BlockSpec(memory_space=pltpu.SMEM), pl.BlockSpec(memory_space=pl.ANY)],
        out_specs=vmem,
        scratch_shapes=[
            pltpu.VMEM((2, *block), f32),
            pltpu.VMEM((2, *block), f32),
            pltpu.VMEM((4, *block), f32),
            pltpu.SemaphoreType.DMA((8 * CHUNKS,)),
            pltpu.SemaphoreType.DMA((8 * CHUNKS,)),
        ],
        compiler_params=pltpu.CompilerParams(collective_id=1, has_side_effects=True, vmem_limit_bytes=24 << 20),
        cost_estimate=pl.CostEstimate(flops=10**6, bytes_accessed=10**7, transcendentals=0),
    )(weights, green)


def cmul(a, b):
    return (a[0] * b[0] - a[1] * b[1], a[0] * b[1] + a[1] * b[0])


def csub(a, b):
    return (a[0] - b[0], a[1] - b[1])


def cadd(a, b):
    return (a[0] + b[0], a[1] + b[1])


def lane_of(x, l):
    return tuple(jnp.broadcast_to(a[:, l : l + 1], VREG) for a in x)


def inv2(p00, p01, p10, p11):
    det = csub(cmul(p00, p11), cmul(p01, p10))
    d = 1.0 / (det[0] * det[0] + det[1] * det[1])
    q = (det[0] * d, -det[1] * d)
    return cmul(p11, q), cmul(p01, q), cmul(p10, q), cmul(p00, q)


class Rows:
    def __init__(self, ref):
        self.ref, self.next, self.kept = ref, 0, {}

    def __call__(self, x, j):
        out = []
        for a in x:
            if id(a) not in self.kept:
                slot = self.next
                self.next = (slot + 1) % SLOTS
                self.ref[slot * 8 : slot * 8 + 8, :] = a
                self.kept[id(a)] = (slot, a)
            slot = self.kept[id(a)][0]
            out.append(self.ref[pl.ds(slot * 8 + j, 8, stride=0), :])
        return tuple(out)


def eliminate_rows(W, t, o, rows_of):
    nv = len(W[0])
    ln = lax.broadcasted_iota(jnp.int32, VREG, 1)
    sb = lax.broadcasted_iota(jnp.int32, VREG, 0)
    el = lambda c, j: rows_of(c[j // 8], j % 8)
    c0 = [lane_of(W[t][v], o) for v in range(nv)]
    c1 = [lane_of(W[t][v], o + 1) for v in range(nv)]
    D = inv2(el(c0, 0), el(c1, 0), el(c0, 1), el(c1, 1))
    for j in range(0, 8 * nv, 2):
        l = o + j
        i00, n01, n10, i11 = D
        ar = ln == l
        ab = ar | (ln == l + 1)

        def rows_in(v, X, s0, s1):
            if j // 8 != v:
                return X
            return tuple(jnp.where(sb == j % 8, s0[k], jnp.where(sb == j % 8 + 1, s1[k], X[k])) for k in range(2))

        last = j + 2 == 8 * nv
        if not last:
            nxt, pivot = [], []
            for ahead in (l + 2, l + 3):
                d = [lane_of(W[t][v], ahead) for v in range(nv)]
                a, c = el(d, j), el(d, j + 1)
                s0 = csub(cmul(i00, a), cmul(n01, c))
                s1 = csub(cmul(i11, c), cmul(n10, a))
                for k in (j + 2, j + 3):
                    pivot.append(csub(el(d, k), cadd(cmul(el(c0, k), s0), cmul(el(c1, k), s1))))
                nxt.append(
                    [rows_in(v, csub(d[v], cadd(cmul(c0[v], s0), cmul(c1[v], s1))), s0, s1) for v in range(nv)]
                )
            D = inv2(pivot[0], pivot[2], pivot[1], pivot[3])
        new = []
        for s in range(2):
            r0 = rows_of(W[s][j // 8], j % 8)
            r1 = rows_of(W[s][(j + 1) // 8], (j + 1) % 8)
            if s == t:
                r0 = (jnp.where(ab, jnp.where(ar, 1.0, 0.0), r0[0]), jnp.where(ab, 0.0, r0[1]))
                r1 = (jnp.where(ab, jnp.where(ar, 0.0, 1.0), r1[0]), jnp.where(ab, 0.0, r1[1]))
            s0 = csub(cmul(i00, r0), cmul(n01, r1))
            s1 = csub(cmul(i11, r1), cmul(n10, r0))
            col = []
            for v in range(nv):
                X = W[s][v]
                if s == t:
                    X = (jnp.where(ab, 0.0, X[0]), jnp.where(ab, 0.0, X[1]))
                col.append(rows_in(v, csub(X, cadd(cmul(c0[v], s0), cmul(c1[v], s1))), s0, s1))
            new.append(col)
        W = new
        if not last:
            c0, c1 = nxt
    return W


def eliminate_rows_of_two(W, t, o, rows_of):
    nv = len(W[0])
    ln = lax.broadcasted_iota(jnp.int32, VREG, 1)
    sb = lax.broadcasted_iota(jnp.int32, VREG, 0)
    el = lambda c, j: rows_of(c[j // 8], j % 8)
    c0 = {0: lane_of(W[t][0], o)}
    c1 = {0: lane_of(W[t][0], o + 1)}
    D = inv2(el(c0, 0), el(c1, 0), el(c0, 1), el(c1, 1))
    for j in range(0, 8 * nv, 2):
        l = o + j
        c0 = [lane_of(W[t][v], l) for v in range(nv)]
        c1 = [lane_of(W[t][v], l + 1) for v in range(nv)]
        i00, n01, n10, i11 = D
        ar = ln == l
        ab = ar | (ln == l + 1)
        new = []
        for s in range(2):
            r0 = rows_of(W[s][j // 8], j % 8)
            r1 = rows_of(W[s][(j + 1) // 8], (j + 1) % 8)
            if s == t:
                r0 = (jnp.where(ab, jnp.where(ar, 1.0, 0.0), r0[0]), jnp.where(ab, 0.0, r0[1]))
                r1 = (jnp.where(ab, jnp.where(ar, 0.0, 1.0), r1[0]), jnp.where(ab, 0.0, r1[1]))
            s0 = csub(cmul(i00, r0), cmul(n01, r1))
            s1 = csub(cmul(i11, r1), cmul(n10, r0))
            col = []
            for v in range(nv):
                X = W[s][v]
                if s == t:
                    X = (jnp.where(ab, 0.0, X[0]), jnp.where(ab, 0.0, X[1]))
                X = csub(X, cadd(cmul(c0[v], s0), cmul(c1[v], s1)))
                if j // 8 == v:
                    X = tuple(
                        jnp.where(sb == j % 8, s0[k], jnp.where(sb == j % 8 + 1, s1[k], X[k])) for k in range(2)
                    )
                col.append(X)
            new.append(col)
        if j + 2 < 8 * nv:
            vs = sorted({j // 8, (j + 2) // 8})
            pivot = []
            for ahead in (l + 2, l + 3):
                d = {v: lane_of(W[t][v], ahead) for v in vs}
                a, c = el(d, j), el(d, j + 1)
                s0 = csub(cmul(i00, a), cmul(n01, c))
                s1 = csub(cmul(i11, c), cmul(n10, a))
                for k in (j + 2, j + 3):
                    pivot.append(csub(el(d, k), cadd(cmul(el(c0, k), s0), cmul(el(c1, k), s1))))
            D = inv2(pivot[0], pivot[2], pivot[1], pivot[3])
        W = new
    return W


def halves(x):
    high = x.astype(bf16)
    return high, (x - high.astype(f32)).astype(bf16)


def dot(a, b):
    return jnp.dot(a, b, preferred_element_type=f32)


def stacked(parts, axis):
    return jnp.concatenate(parts, axis)


def left_panel(M, o):
    ln = lax.broadcasted_iota(jnp.int32, M[0].shape, 1)
    here = (ln >= o) & (ln < o + SUB)
    both = jnp.where(here, M[0], 0.0) + pltpu.roll(jnp.where(here, M[1], 0.0), SUB, 1)
    high = both.astype(bf16).astype(f32)
    low = both - high
    return stacked([(high + pltpu.roll(low, 2 * SUB, 1)).astype(bf16), high.astype(bf16)], 1)


def right_panel(W, o):
    re = stacked([stacked([W[s][v][0] for v in range(4)], 0) for s in range(2)], 1)
    im = stacked([stacked([W[s][v][1] for v in range(4)], 0) for s in range(2)], 1)
    (rh, rl), (ih, il) = halves(re), halves(im)
    top_h, bottom_h = stacked([rh, ih], 1), stacked([-ih, rh], 1)
    top_l, bottom_l = stacked([rl, il], 1), stacked([-il, rl], 1)
    none = jnp.zeros((SUB, 2 * N), bf16)
    first = [top_h, bottom_h, top_h, bottom_h]
    second = [top_l, bottom_l, none, none]
    turn = o // SUB
    around = lambda x: [x[(g - turn) % 4] for g in range(4)]
    return stacked(around(first) + around(second), 0)


def invert(mats, rows_of, beside=None):
    def tile_steps(tile, carry):
        columns = [pl.ds(pl.multiple_of(128 * tile, 128), 128), pl.ds(pl.multiple_of(128 - 128 * tile, 128), 128)]
        rows_of.kept.clear()
        if beside is not None:
            beside(tile)
        eliminate = eliminate_rows if len(mats) == 1 else eliminate_rows_of_two

        def rows(q, height):
            return pl.ds(pl.multiple_of(128 * tile + SUB * q, SUB), height)

        panels = []
        for M in mats:
            whole = [[M[k][rows(0, SUB), c] for k in range(2)] for c in columns]
            panels.append([[tuple(x[8 * v : 8 * v + 8] for x in w) for v in range(4)] for w in whole])
        ln = lax.broadcasted_iota(jnp.int32, (N, 128), 1)
        for q in range(4):
            o = q * SUB
            here = (ln >= o) & (ln < o + SUB)
            lefts = [left_panel([M[k][:, columns[0]] for k in range(2)], o) for M in mats]
            strips = [left_panel([M[k][rows((q + 1) % 4, SUB), columns[0]] for k in range(2)], o) for M in mats]
            panels = [eliminate(W, 0, o, rows_of) for W in panels]
            following = []
            for M, L, W in zip(mats, lefts, panels):
                R = right_panel(W, o)
                if q < 3:
                    U = dot(strips.pop(0), R)
                    nxt = []
                    for s, c in enumerate(columns):
                        pairs = []
                        for k in range(2):
                            X = M[k][rows(q + 1, SUB), c]
                            if s == 0:
                                X = jnp.where(here[:SUB], 0.0, X)
                            pairs.append(X - U[:, k * N + s * 128 : k * N + s * 128 + 128])
                        nxt.append([tuple(x[8 * v : 8 * v + 8] for x in pairs) for v in range(4)])
                    following.append(nxt)
                U = dot(L, R)
                for s, c in enumerate(columns):
                    for k in range(2):
                        X = M[k][:, c]
                        if s == 0:
                            X = jnp.where(here, 0.0, X)
                        M[k][:, c] = X - U[:, k * N + s * 128 : k * N + s * 128 + 128]
                        M[k][rows(q, SUB), c] = stacked([W[s][v][k] for v in range(4)], 0)
            panels = following
        return carry

    lax.fori_loop(0, 2, tile_steps, 0)


def product(A, B):
    ah, al = halves(stacked([A[0], A[1]], 1))
    (rh, rl), (ih, il) = halves(B[0]), halves(B[1])
    bh = stacked([stacked([rh, ih], 1), stacked([-ih, rh], 1)], 0)
    bl = stacked([stacked([rl, il], 1), stacked([-il, rl], 1)], 0)
    C = dot(ah, bh) + (dot(ah, bl) + dot(al, bh))
    return C[:, :N], C[:, N:]


def planes(ref):
    return ref.at[0], ref.at[1]


def pair(ref):
    re, im = planes(ref)
    return re[...], im[...]


def put(ref, x):
    re, im = ref if isinstance(ref, tuple) else planes(ref)
    re[...], im[...] = x


def green_kernel(
    energy_ref, broadening_ref, contact_ref, offset_ref, weight_ref, herm_ref, hop_ref, out_ref, reach_ref, kept_ref,
    bank, work, scr,
):
    rows_of = Rows(scr)
    place = lax.axis_index("space")
    point, points = lax.axis_index("energy"), lax.axis_size("energy")
    side = place // 2
    e, eta, c = energy_ref[0], broadening_ref[0], contact_ref[0]

    even = lax.rem(point, 2) == 0
    reach = [-2, 2, -4, 4] + [jnp.where(even, a, b) for a, b in ((1, -1), (-1, -3), (3, 1), (-3, 3))]
    for k, d in enumerate(reach):
        inside = (point + d >= 0) & (point + d < points)
        total = jnp.float32(0.0)
        for j in range(8):
            total = total + jnp.where(inside & (offset_ref[0, j] == d), weight_ref[0, j], 0.0)
        reach_ref[k] = total

    row, column = triangles()
    eye = (row == column).astype(f32)

    def herm(k):
        mixed = herm_ref[k]
        turned = mixed.T
        return (
            jnp.where(row <= column, mixed, turned),
            jnp.where(row > column, mixed, jnp.where(row < column, -turned, 0.0)),
        )

    hop = lambda k: (hop_ref[k, 0], hop_ref[k, 1])
    back = lambda k: (hop_ref[k, 0].T, -hop_ref[k, 1].T)

    gram = product(hop(0), back(0))
    h0, h3 = herm(0), herm(3)
    put(planes(bank.at[0]), (e * eye - h0[0] - c * gram[1], eta * eye - h0[1] + c * gram[0]))
    put(planes(bank.at[1]), (e * eye - h3[0], (eta + c) * eye - h3[1]))
    put(planes(bank.at[2]), back(1))
    put(planes(bank.at[3]), hop(1))
    put(planes(bank.at[4]), hop(3))
    put(planes(bank.at[5]), back(3))

    @pl.when(side == 0)
    def _():
        put(planes(bank.at[6]), hop(2))
        put(planes(bank.at[7]), back(2))

    @pl.when(side == 1)
    def _():
        put(planes(bank.at[6]), back(2))
        put(planes(bank.at[7]), hop(2))

    invert([planes(bank.at[0]), planes(bank.at[1])], rows_of)

    def inner(i, sigma):
        h = herm(i)
        return (e * eye - h[0] - sigma[0], eta * eye - h[1] - sigma[1])

    far = 1 - side
    near_l, near_r = 2 + 2 * side, 3 + 2 * side
    right = product(pair(bank.at[far]), pair(bank.at[2 * far + 3]))
    put(work, inner(1 + far, product(pair(bank.at[2 * far + 2]), right)))

    def solve(step, carry):
        def near_product(tile):
            job = 2 * step + tile
            first = jnp.where(job == 0, side, near_l)
            second = jnp.where(job == 0, near_r, jnp.where(job == 1, 8, side))
            put(bank.at[jnp.where(job == 0, 8, jnp.where(job == 1, 9, 10))], product(pair(bank.at[first]), pair(bank.at[second])))

        invert([planes(work)], rows_of, near_product)

        @pl.when(step == 0)
        def _():
            right = product(pair(work), pair(bank.at[7]))
            middle = product(pair(bank.at[6]), right)
            put(work, inner(1 + side, cadd(pair(bank.at[9]), middle)))

        return carry

    lax.fori_loop(0, 2, solve, 0)

    def finish(x):
        put(out_ref, x)
        put(kept_ref, x)

    @pl.when((place == 1) | (place == 2))
    def _():
        finish(pair(work))

    @pl.when((place == 0) | (place == 3))
    def _():
        finish(cadd(pair(bank.at[side]), product(pair(bank.at[8]), product(pair(work), pair(bank.at[10])))))


def green_block(energy, broadening, contact, offset, weight, herms, hops):
    vmem = pl.BlockSpec(memory_space=pltpu.VMEM)
    smem = pl.BlockSpec(memory_space=pltpu.SMEM)
    block = pltpu.VMEM((2, N, N), f32)
    return pl.pallas_call(
        green_kernel,
        out_shape=(
            jax.ShapeDtypeStruct((2, N, N), f32),
            jax.ShapeDtypeStruct((8,), f32),
            jax.ShapeDtypeStruct((2, N, N), f32),
        ),
        in_specs=[smem] * 5 + [vmem] * 2,
        out_specs=(vmem, smem, vmem),
        scratch_shapes=[
            pltpu.VMEM((11, 2, N, N), f32),
            block,
            pltpu.VMEM((8 * SLOTS, 128), f32),
        ],
        compiler_params=pltpu.CompilerParams(vmem_limit_bytes=48 << 20),
        cost_estimate=pl.CostEstimate(flops=10**10, bytes_accessed=10**7, transcendentals=0),
    )(energy, broadening, contact, offset, weight, herms, hops)


def per_device(ham_blocks, hopping, energy, broadening, contact, phonon_offset, phonon_weight):
    herms, hops = gathered(ham_blocks[0], hopping[0])
    green, reach, kept = green_block(energy, broadening, contact, phonon_offset, phonon_weight, herms, hops)
    total = phonon_sum(reach, kept.reshape(512, N)).reshape(2, N, N)
    return (green[None, None], total[None, None])


def solution(mesh):
    placed = (
        P("space", None, None, None),
        P("space", None, None, None),
        P("energy"),
        P("energy"),
        P("energy"),
        P("energy", None),
        P("energy", None),
    )
    return jax.shard_map(
        per_device,
        mesh=mesh,
        in_specs=placed,
        out_specs=(P("energy", "space", None, None, None), P("energy", "space", None, None, None)),
        check_vma=False,
    )
```
